256 devices in a mesh: wide: 32 (over y, z_hi, core), narrow: 8 (over z_lo, x).
Axes of the slice: x: 4, y: 4, z: 8 (z_hi: 4, z_lo: 2; z = z_hi * 2 + z_lo), core: 2. Of those that a mesh axis runs over, the one named last changes fastest.
Arguments:
- images: bfloat16 [24576, 512], P('wide'), may hold values from -20 to 20
- captions: bfloat16 [24576, 512], P(('wide', 'narrow')), may hold values from -20 to 20
- taxon_paths: int32 [7, 24576], P(None, 'wide'), may hold values from 0 to 2047, as said below
- sample_weight: float32 [24576], P('wide'), may hold values from 2 to 20
- depth_weight: float32 [8], replicated, may hold values from 0.1 to 10
Outputs:
- grad_images: float32 [24576, 512], P(('wide', 'narrow'))
- grad_captions: float32 [24576, 512], P(('wide', 'narrow'))
The draws below stay inside these ranges and needn't reach their ends.
Inputs may be any that keep to these rules, and one draw needn't show every extreme that they name: `taxon_paths`: A taxon id at one rank determines the ids at all ranks before it.
All inputs are finite; a program needn't handle non-finite values.
Results may differ from the reference program's by a relative error of at most 0.0039.
Values may be sent and summed in bfloat16 or wider, within the bound.
A program may use at most 128 MiB of HBM per device.

```python
import math
import jax
import jax.numpy as jnp
from jax import lax

EMBED = 512
RANKS = 7
DEPTHS = 8
ROWS = 768
TOKENS = 24576


def normal_base(key):
    return jnp.clip(jax.random.normal(key, (TOKENS, EMBED), jnp.float32), -4.0, 4.0)


def draw_captions(key, part):
    shared = normal_base(key)
    return shared.astype(jnp.bfloat16)


def draw_images(key, part):
    key = jax.random.fold_in(key, 7)
    own_key, scale_key = jax.random.split(key)
    own = jnp.clip(jax.random.normal(own_key, (TOKENS, EMBED), jnp.float32), -4.0, 4.0)
    row_scale = jnp.exp(jax.random.uniform(scale_key, (TOKENS, 1), jnp.float32, math.log(0.3), math.log(3.0)))
    result = own * row_scale
    return result.astype(jnp.bfloat16)


def draw_taxon_paths(key, part):
    key = jax.random.fold_in(key, 9)
    branchings = [2, 2, 2, 4, 4, 4, 4]
    prefix = jnp.zeros((TOKENS,), jnp.int32)
    levels = []
    for rank_level in range(RANKS):
        branch_pick = jax.random.randint(jax.random.fold_in(key, rank_level), (TOKENS,), 0, branchings[rank_level], jnp.int32)
        prefix = prefix * branchings[rank_level] + branch_pick
        levels.append(prefix)
    return jnp.stack(levels)


def block_scale(key, dims, cuts, low, high):
    loudness, own = 1.0, jax.random.fold_in(key, 6)
    for position, shards_of in cuts:
        steps = jnp.exp(jax.random.uniform(jax.random.fold_in(own, position), (shards_of,), jnp.float32, low / len(cuts), high / len(cuts)))
        loudness = loudness * jnp.repeat(steps, dims[position] // shards_of).reshape([-1 if axis == position else 1 for axis in range(len(dims))])
    return loudness


def setup_inputs(seed: int = 0) -> dict:
    keys = jax.random.split(jax.random.key(seed), 6)
    images = draw_images(jax.random.fold_in(keys[5], 71), 0)
    captions = draw_captions(jax.random.fold_in(keys[5], 71), 0)
    taxon_paths = draw_taxon_paths(jax.random.fold_in(keys[5], 71), 0)
    sample_weight = jnp.clip(jnp.exp(math.log(20.0) - 2.3025851 * jax.random.uniform(keys[3], (TOKENS,), jnp.float32) ** block_scale(keys[3], (TOKENS,), ((0, 32),), -0.2, 0.2)), 2.0, 20.0)
    depth_weight = jnp.clip(jnp.exp(jax.random.uniform(keys[4], (DEPTHS,), jnp.float32, math.log(0.1), math.log(10.0))), 0.1, 10.0)
    return dict(images=images, captions=captions, taxon_paths=taxon_paths, sample_weight=sample_weight, depth_weight=depth_weight)


def pair_weights(image_paths, caption_paths, depth_weight):
    matched = jnp.ones((image_paths.shape[1], caption_paths.shape[1]), jnp.bool_)
    depth_count = jnp.zeros(matched.shape, jnp.int32)
    for rank_level in range(image_paths.shape[0]):
        same_id = image_paths[rank_level][:, None] == caption_paths[rank_level][None, :]
        matched = jnp.logical_and(matched, same_id)
        depth_count = depth_count + matched.astype(jnp.int32)
    weights = jnp.zeros(depth_count.shape, jnp.float32)
    for depth_level in range(depth_weight.shape[0]):
        weights = weights + jnp.where(depth_count == depth_level, depth_weight[depth_level], 0.0)
    return weights


def reference(images, captions, taxon_paths, sample_weight, depth_weight):
    score_scale = EMBED ** -0.5
    blocks = TOKENS // ROWS
    image_blocks = images.reshape(blocks, ROWS, EMBED)
    path_blocks = taxon_paths.reshape(RANKS, blocks, ROWS).transpose(1, 0, 2)
    weight_blocks = sample_weight.reshape(blocks, ROWS)

    def block_step(grad_caps, inputs):
        block_images, block_paths, block_weight = inputs
        scores = score_scale * jnp.dot(block_images, captions.T, preferred_element_type=jnp.float32)
        row_peak = jnp.max(scores, axis=1, keepdims=True)
        exp_scores = jnp.exp(scores - row_peak)
        row_total = jnp.sum(exp_scores, axis=1, keepdims=True)
        target = pair_weights(block_paths, taxon_paths, depth_weight)
        weight_total = jnp.sum(target, axis=1, keepdims=True)
        soft_values = exp_scores.astype(jnp.bfloat16)
        taught = target.astype(jnp.bfloat16)
        weighted = jnp.dot(soft_values, captions, preferred_element_type=jnp.float32)
        teach = jnp.dot(taught, captions, preferred_element_type=jnp.float32)
        row_factor = block_weight[:, None]
        grad_block = score_scale * row_factor * (weighted / row_total - teach / weight_total)
        grad_scores = (row_factor * (exp_scores / row_total - target / weight_total)).astype(jnp.bfloat16)
        grad_caps = grad_caps + score_scale * jnp.dot(grad_scores.T, block_images, preferred_element_type=jnp.float32)
        return grad_caps, grad_block

    grad_caps, grad_blocks = lax.scan(block_step, jnp.zeros((TOKENS, EMBED), jnp.float32), (image_blocks, path_blocks, weight_blocks))
    return grad_blocks.reshape(TOKENS, EMBED), grad_caps
```

```python
import functools
import math

import jax
import jax.numpy as jnp
from jax import lax
from jax.experimental import pallas as pl
from jax.experimental.pallas import tpu as pltpu
from jax.sharding import PartitionSpec as P

BF16, F32 = jnp.bfloat16, jnp.float32
NY, NH, NX, NL = 4, 4, 4, 2
ARRIVE = (0, 3, 1, 2)
LEAVE = (2, 1, 3, 0)


def kernel(
    img_ref, cap_ref, tax_ref, sw_ref, dw_ref, gi_ref, gc_ref,
    caps, img_t, ids, e_buf, t_buf, e_low, t_low, acc_e, acc_t, peaks, stat_out, stat_in,
    p_own, p_out, p_in, a_out, a_in, b_out, b_in, za_out, za_in, zb_out, zb_in,
    x_out, x_in, l_out, l_in,
    cap_send, cap_recv, id_send, id_recv, stat_send, stat_recv,
    p_send, p_recv, a_send, a_recv, b_send, b_recv, za_send, za_recv, zb_send, zb_recv,
    x_send, x_recv, l_send, l_recv,
):
    rows, width = img_ref.shape
    own = cap_ref.shape[0]
    half = own // 2
    pair = 2 * own
    ranks = tax_ref.shape[0]
    scale = width ** -0.5
    to_exp2 = scale * math.log2(math.e)

    wide, narrow = lax.axis_index("wide"), lax.axis_index("narrow")
    core, h, y = wide % 2, (wide // 2) % NH, wide // (2 * NH)
    x, low = narrow % NX, narrow // NX

    def chip(dy, dh):
        return ((y + dy) % NY) * NH + (h + dh) % NH

    def slot(dy, dh, dc=0):
        return chip(dy, dh) * 2 + (core + dc) % 2

    def at_wide(dy, dh, dc=0):
        return {"wide": slot(dy, dh, dc)}

    def at_narrow(dx, dl):
        return {"narrow": ((low + dl) % NL) * NX + (x + dx) % NX}

    barrier = pltpu.get_barrier_semaphore()
    partners = [at_wide(0, 0, 1)]
    partners += [at_wide(0, d) for d in range(1, NH)] + [at_wide(d, 0) for d in range(1, NY)]
    partners += [at_narrow(dx, dl) for dl in range(NL) for dx in range(NX) if dx or dl]
    for partner in partners:
        pl.semaphore_signal(barrier, inc=1, device_id=partner, device_id_type=pl.DeviceIdType.MESH)

    sent = []

    def send(src, dst, send_sem, recv_sem, where):
        copy = pltpu.make_async_remote_copy(
            src_ref=src, dst_ref=dst, send_sem=send_sem, recv_sem=recv_sem,
            device_id=where, device_id_type=pl.DeviceIdType.MESH,
        )
        copy.start()
        sent.append(copy)

    def arrived(dst, recv_sem):
        pltpu.make_async_copy(dst, dst, recv_sem).wait()

    caps[pl.ds(wide, 1)] = cap_ref[...][None]
    all_ids = jnp.concatenate([tax_ref[...], jnp.zeros((8 - ranks, rows), jnp.int32)], axis=0)
    own_ids = pltpu.roll(all_ids, (rows - own * narrow) % rows, 1)[:, :128]
    ids[pl.ds(wide, 1)] = own_ids[None]

    pl.semaphore_wait(barrier, len(partners))

    cap_sends = iter(range(64))

    def send_caps(s, where, begin=0, size=own):
        k = next(cap_sends)
        piece = caps.at[s, pl.ds(begin, size)]
        send(piece, piece, cap_send.at[k], cap_recv.at[s], where)

    def caps_arrived(s):
        arrived(caps.at[s], cap_recv.at[s])

    mine = ids.at[pl.ds(wide, 1)]
    send(mine, mine, id_send.at[0], id_recv.at[0], at_wide(0, 0, 1))
    send_caps(wide, at_wide(1, 0))
    send_caps(wide, at_wide(3, 0))
    send_caps(wide, at_wide(0, 1))
    send_caps(wide, at_wide(0, 3))
    send_caps(wide, at_wide(0, 0, 1))
    other = ids.at[pl.ds(slot(0, 0, 1), 1)]
    arrived(other, id_recv.at[0])
    both = ids.at[pl.ds(2 * chip(0, 0), 2)]
    for d in range(1, NH):
        send(both, both, id_send.at[d], id_recv.at[NH - d], at_wide(0, d))

    img_t[...] = img_ref[...].T
    peaks[...] = jnp.full_like(peaks, -jnp.inf)

    for d in range(1, NH):
        theirs = ids.at[pl.ds(2 * chip(0, d), 2)]
        arrived(theirs, id_recv.at[d])
    column = ids.at[pl.ds(2 * NH * y, 2 * NH)]
    for d in range(1, NY):
        send(column, column, id_send.at[NH - 1 + d], id_recv.at[NH - 1 + NY - d], at_wide(d, 0))

    def targets(dh, first, count, total):
        def step(i, total):
            dy, c = first + i // 2, i % 2
            g = chip(dy, dh)
            turned = ids[2 * g + c].T
            for r in range(0, own, 32):
                weight = jnp.full((32, rows), dw_ref[0], F32)
                for k in range(ranks):
                    same = turned[r : r + 32, k : k + 1] == tax_ref[k : k + 1, :]
                    weight = jnp.where(same, dw_ref[k + 1], weight)
                t_buf[g, pl.ds(c * own + r, 32), :] = weight
                t_low[dh, dy, pl.ds(c * own + r, 32), :] = weight.astype(BF16)
                total = total + jnp.sum(weight.reshape(4, 8, rows), axis=0)
            return total

        return lax.fori_loop(0, 2 * count, step, total)

    def scores(dh, order, peak, total):
        def product(dy, biggest):
            g = chip(dy, dh)
            block = caps[pl.ds(2 * g, 2)].reshape(pair, width)
            s = jnp.dot(block, img_t[...], preferred_element_type=F32)
            e_buf[g] = s
            return jnp.maximum(biggest, jnp.max(s.reshape(pair // 8, 8, rows), axis=0))

        biggest = lax.fori_loop(0, NY, product, jnp.broadcast_to(peak, (8, rows)))
        new_peak = jnp.max(biggest, axis=0, keepdims=True)
        shrink = jnp.exp2((peak - new_peak) * to_exp2)

        def exponentials(dy, part):
            g = chip(dy, dh)
            e = jnp.exp2((e_buf[g] - new_peak) * to_exp2)
            e_buf[g] = e
            e_low[dy] = e.astype(BF16)
            return part + jnp.sum(e.reshape(pair // 8, 8, rows), axis=0)

        part = lax.fori_loop(0, NY, exponentials, jnp.zeros((8, rows), F32))
        peaks[pl.ds(order, 1)] = new_peak
        return new_peak, shrink, total * shrink + jnp.sum(part, axis=0, keepdims=True)

    def moments(dh, shrink, first):
        block = jnp.concatenate(
            [caps[pl.ds(2 * chip(dy, dh), 2)].reshape(pair, width) for dy in range(NY)], axis=0
        )
        turned = block.T
        for j in range(0, rows, 256):
            cut = slice(j, j + 256)
            new_e = jnp.dot(turned, e_low[:, :, cut].reshape(NY * pair, 256), preferred_element_type=F32)
            new_t = jnp.dot(turned, t_low[dh, :, :, cut].reshape(NY * pair, 256), preferred_element_type=F32)
            if first:
                acc_e[:, cut] = new_e
                acc_t[:, cut] = new_t
            else:
                acc_e[:, cut] = acc_e[:, cut] * shrink[:, cut] + new_e
                acc_t[:, cut] = acc_t[:, cut] + new_t

    def column_in(dh):
        s = slot(0, dh)
        caps_arrived(s)
        send_caps(s, at_wide(1, 0))
        send_caps(s, at_wide(3, 0))
        if dh == 3:
            send_caps(s, at_wide(0, 1), 0, half)
        if dh == 1:
            send_caps(s, at_wide(0, 3), half, half)
        send_caps(s, at_wide(0, 0, 1))

    def sides_in(dh):
        for dy, on, begin in ((3, 1, 0), (1, 3, half)):
            s = slot(dy, dh)
            caps_arrived(s)
            send_caps(s, at_wide(on, 0), begin, half)
            send_caps(s, at_wide(0, 0, 1))

    def far_in(dh):
        s = slot(2, dh)
        caps_arrived(s)
        send_caps(s, at_wide(0, 0, 1))

    def others_in(dh):
        for dy in range(NY):
            caps_arrived(slot(dy, dh, 1))

    peak = jnp.full((1, rows), -jnp.inf, F32)
    exp_total = jnp.zeros((1, rows), F32)
    t_total = jnp.zeros((8, rows), F32)

    for order, dh in enumerate(ARRIVE):
        if order == 0:
            t_total = targets(dh, 0, 1, t_total)
        sides_in(dh)
        if order == 0:
            column_in(3)
            column_in(1)
            for d in range(1, NY):
                theirs = ids.at[pl.ds(2 * NH * ((y + d) % NY), 2 * NH)]
                arrived(theirs, id_recv.at[NH - 1 + d])
            t_total = targets(dh, 1, NY - 1, t_total)
        if order == 1:
            column_in(2)
        far_in(dh)
        others_in(dh)
        peak, shrink, exp_total = scores(dh, order, peak, exp_total)
        if order < NH - 1:
            t_total = targets(ARRIVE[order + 1], 0, NY, t_total)
            moments(dh, shrink, order == 0)

    stat_out[...] = jnp.concatenate(
        [peak, exp_total, jnp.sum(t_total, axis=0, keepdims=True), jnp.zeros((5, rows), F32)], axis=0
    )
    k = 0
    for dl in range(NL):
        for dx in range(NX):
            if dx or dl:
                back = ((NL - dl) % NL) * NX + (NX - dx) % NX
                send(stat_out, stat_in.at[back], stat_send.at[k], stat_recv.at[back], at_narrow(dx, dl))
                k += 1
    moments(ARRIVE[-1], shrink, False)
    for k in range(1, NL * NX):
        arrived(stat_in.at[k], stat_recv.at[k])
    stats = [stat_out[...]] + [stat_in[k] for k in range(1, NL * NX)]
    top = functools.reduce(jnp.maximum, [s[0:1] for s in stats])
    exp_all = sum(s[1:2] * jnp.exp2((s[0:1] - top) * to_exp2) for s in stats)
    t_all = sum(s[2:3] for s in stats)
    factor_e = sw_ref[...] / exp_all
    factor_t = sw_ref[...] / t_all

    def terms(dy, dh):
        g, k = chip(dy, dh), dy * NH + dh
        to_e = factor_e * jnp.exp2((peaks[ARRIVE.index(dh) : ARRIVE.index(dh) + 1] - top) * to_exp2)
        grad = (to_e * e_buf[g] - factor_t * t_buf[g]).astype(BF16)
        p_own[k] = scale * jnp.dot(grad, img_ref[...], preferred_element_type=F32)
        p_out[k] = p_own[k, pl.ds((1 - core) * own, own), :].astype(BF16)
        send(p_out.at[k], p_in.at[k], p_send.at[k], p_recv.at[k], at_wide(0, 0, 1))

    def chip_sum(dy, dh):
        k = dy * NH + dh
        arrived(p_in.at[k], p_recv.at[k])
        return p_own[k, pl.ds(core * own, own), :] + p_in[k].astype(F32)

    def finish(dy, dh):
        value = chip_sum(dy, dh)
        if dy == 2:
            a_out[dh] = value.astype(BF16)
            for side, (begin, on) in enumerate(((0, 1), (half, 3))):
                cut = pl.ds(begin, half)
                send(a_out.at[dh, cut], a_in.at[dh, cut], a_send.at[dh, side], a_recv.at[dh, side], at_wide(on, 0))
        elif dy in (1, 3):
            side = 0 if dy == 1 else 1
            cut = pl.ds(side * half, half)
            arrived(a_in.at[dh, cut], a_recv.at[dh, side])
            gained = a_in[dh, side * half : (side + 1) * half].astype(F32)
            parts = [value[:half], value[half:]]
            parts[side] = parts[side] + gained
            b_out[dh, side] = jnp.concatenate(parts, axis=0).astype(BF16)
            send(b_out.at[dh, side], b_in.at[dh, side], b_send.at[dh, side], b_recv.at[dh, side], at_wide(dy, 0))
        else:
            for side in (0, 1):
                arrived(b_in.at[dh, side], b_recv.at[dh, side])
                value = value + b_in[dh, side].astype(F32)
            if dh == 2:
                za_out[...] = value.astype(BF16)
                for side, (begin, on) in enumerate(((0, 1), (half, 3))):
                    cut = pl.ds(begin, half)
                    send(za_out.at[cut], za_in.at[cut], za_send.at[side], za_recv.at[side], at_wide(0, on))
            elif dh in (1, 3):
                side = 0 if dh == 1 else 1
                arrived(za_in.at[pl.ds(side * half, half)], za_recv.at[side])
                gained = za_in[side * half : (side + 1) * half].astype(F32)
                parts = [value[:half], value[half:]]
                parts[side] = parts[side] + gained
                zb_out[side] = jnp.concatenate(parts, axis=0).astype(BF16)
                send(zb_out.at[side], zb_in.at[side], zb_send.at[side], zb_recv.at[side], at_wide(0, dh))
            else:
                for side in (0, 1):
                    arrived(zb_in.at[side], zb_recv.at[side])
                    value = value + zb_in[side].astype(F32)
                gc_ref[...] = value

    def image_terms():
        own_e = scale * factor_e * jnp.exp2((peak - top) * to_exp2)
        own_t = scale * factor_t
        turned = (acc_e[...] * own_e - acc_t[...] * own_t).T
        x_out[...] = turned.reshape(NL, NX, own, width).astype(BF16)
        for d in range(1, NX):
            to = (x + d) % NX
            send(x_out.at[:, to], x_in.at[NX - d], x_send.at[d], x_recv.at[NX - d], at_narrow(d, 0))

    def image_sum():
        for d in range(1, NX):
            arrived(x_in.at[d], x_recv.at[d])

        def total(which):
            value = x_out[which, x].astype(F32)
            for d in range(1, NX):
                value = value + x_in[d, which].astype(F32)
            return value

        l_out[...] = total(1 - low).astype(BF16)
        send(l_out, l_in, l_send.at[0], l_recv.at[0], at_narrow(0, 1))
        gi_ref[...] = total(low)

    def image_finish():
        arrived(l_in, l_recv.at[0])
        gi_ref[...] = gi_ref[...] + l_in[...].astype(F32)

    steps = [(2, dh) for dh in LEAVE]
    for dh in LEAVE:
        steps += [(1, dh), (3, dh)]
    steps += [(0, dh) for dh in LEAVE]
    lag = 2
    for i, step in enumerate(steps):
        terms(*step)
        if i == 4:
            image_terms()
        if i >= lag:
            finish(*steps[i - lag])
        if i == 13:
            image_sum()
    for step in steps[len(steps) - lag :]:
        finish(*step)
    image_finish()
    for copy in sent:
        copy.wait_send()


def body(images, captions, taxon_paths, sample_weight, depth_weight):
    rows, width = images.shape
    own = captions.shape[0]
    pair, half = 2 * own, own // 2
    ranks = taxon_paths.shape[0]
    slots = 2 * NY * NH
    chips = NY * NH
    vmem = pl.BlockSpec(memory_space=pltpu.VMEM)
    dma = pltpu.SemaphoreType.DMA
    scratch = [
        pltpu.VMEM((slots, own, width), BF16),
        pltpu.VMEM((width, rows), BF16),
        pltpu.VMEM((slots, 8, 128), jnp.int32),
        pltpu.VMEM((chips, pair, rows), F32),
        pltpu.VMEM((chips, pair, rows), F32),
        pltpu.VMEM((NY, pair, rows), BF16),
        pltpu.VMEM((NH, NY, pair, rows), BF16),
        pltpu.VMEM((width, rows), F32),
        pltpu.VMEM((width, rows), F32),
        pltpu.VMEM((8, rows), F32),
        pltpu.VMEM((8, rows), F32),
        pltpu.VMEM((NL * NX, 8, rows), F32),
        pltpu.VMEM((chips, pair, width), F32),
        pltpu.VMEM((chips, own, width), BF16),
        pltpu.VMEM((chips, own, width), BF16),
        pltpu.VMEM((NH, own, width), BF16),
        pltpu.VMEM((NH, own, width), BF16),
        pltpu.VMEM((NH, 2, own, width), BF16),
        pltpu.VMEM((NH, 2, own, width), BF16),
        pltpu.VMEM((own, width), BF16),
        pltpu.VMEM((own, width), BF16),
        pltpu.VMEM((2, own, width), BF16),
        pltpu.VMEM((2, own, width), BF16),
        pltpu.VMEM((NL, NX, own, width), BF16),
        pltpu.VMEM((NX, NL, own, width), BF16),
        pltpu.VMEM((own, width), BF16),
        pltpu.VMEM((own, width), BF16),
        dma((64,)), dma((slots,)), dma((8,)), dma((8,)), dma((8,)), dma((8,)),
        dma((chips,)), dma((chips,)), dma((NH, 2)), dma((NH, 2)), dma((NH, 2)), dma((NH, 2)),
        dma((2,)), dma((2,)), dma((2,)), dma((2,)),
        dma((NX,)), dma((NX,)), dma((1,)), dma((1,)),
    ]
    out = jax.ShapeDtypeStruct((own, width), F32)
    pairs = slots * own * rows
    return pl.pallas_call(
        kernel,
        out_shape=(out, out),
        in_specs=[vmem, vmem, vmem, vmem, pl.BlockSpec(memory_space=pltpu.SMEM)],
        out_specs=(vmem, vmem),
        scratch_shapes=scratch,
        compiler_params=pltpu.CompilerParams(
            collective_id=0, has_side_effects=True, vmem_limit_bytes=58 * 1024 * 1024
        ),
        cost_estimate=pl.CostEstimate(
            flops=8 * pairs * width, bytes_accessed=4 * rows * width, transcendentals=pairs
        ),
    )(images, captions, taxon_paths, sample_weight.reshape(1, rows), depth_weight)


def solution(mesh):
    return jax.shard_map(
        body,
        mesh=mesh,
        in_specs=(P("wide", None), P(("wide", "narrow"), None), P(None, "wide"), P("wide"), P()),
        out_specs=(P(("wide", "narrow"), None), P(("wide", "narrow"), None)),
        check_vma=False,
    )
```

```python
import functools
import math

import jax
import jax.numpy as jnp
from jax import lax
from jax.experimental import pallas as pl
from jax.experimental.pallas import tpu as pltpu
from jax.sharding import PartitionSpec as P

BF16, F32 = jnp.bfloat16, jnp.float32
NY, NH, NX, NL = 4, 4, 4, 2
LANES = 128


def id_codes(ids):
    return ((ids & 127) + 128).astype(F32) * jnp.exp2((ids >> 7).astype(F32))


def kernel(
    img_ref, cap_ref, tax_ref, sw_ref, dw_ref, gi_ref, gc_ref,
    caps, img_t, ids, row_codes, col_codes, e_buf, e_low, t_high, t_low, acc_e, acc_t, t_sum, peaks,
    stat_out, stat_in,
    p_own, p_out, p_in, ya_out, ya_in, zs_out, zs_in, yf_out, yf_in, zf_out, zf_in,
    x_out, x_in, l_out, l_in,
    cap_send, cap_recv, id_send, id_recv, stat_send, stat_recv,
    p_send, p_recv, ya_send, ya_recv, zs_send, zs_recv, yf_send, yf_recv, zf_send, zf_recv,
    x_send, x_recv, l_send, l_recv,
):
    rows, width = img_ref.shape
    own = cap_ref.shape[0]
    pair = 2 * own
    ranks = tax_ref.shape[0]
    scale = width ** -0.5
    to_exp2 = scale * math.log2(math.e)

    wide, narrow = lax.axis_index("wide"), lax.axis_index("narrow")
    core, h, y = wide % 2, (wide // 2) % NH, wide // (2 * NH)
    x, low = narrow % NX, narrow // NX
    near, back = 1 + 2 * core, 3 - 2 * core

    def chip(dy, dh):
        return ((y + dy) % NY) * NH + (h + dh) % NH

    def slot(dy, dh, dc=0):
        return chip(dy, dh) * 2 + (core + dc) % 2

    def at_wide(dy, dh, dc=0):
        return {"wide": slot(dy, dh, dc)}

    def at_narrow(dx, dl):
        return {"narrow": ((low + dl) % NL) * NX + (x + dx) % NX}

    barrier = pltpu.get_barrier_semaphore()
    partners = [at_wide(0, 0, 1)]
    partners += [at_wide(0, d) for d in range(1, NH)] + [at_wide(d, 0) for d in range(1, NY)]
    partners += [at_narrow(dx, dl) for dl in range(NL) for dx in range(NX) if dx or dl]
    for partner in partners:
        pl.semaphore_signal(barrier, inc=1, device_id=partner, device_id_type=pl.DeviceIdType.MESH)

    sent = []

    def send(src, dst, send_sem, recv_sem, where):
        copy = pltpu.make_async_remote_copy(
            src_ref=src, dst_ref=dst, send_sem=send_sem, recv_sem=recv_sem,
            device_id=where, device_id_type=pl.DeviceIdType.MESH,
        )
        copy.start()
        sent.append(copy)

    def arrived(dst, recv_sem):
        pltpu.make_async_copy(dst, dst, recv_sem).wait()

    caps[pl.ds(wide, 1)] = cap_ref[...][None]
    own_rows = tax_ref[...]
    all_ids = jnp.concatenate([own_rows, jnp.zeros((8 - ranks, rows), jnp.int32)], axis=0)
    ids[pl.ds(wide, 1)] = pltpu.roll(all_ids, (rows - own * narrow) % rows, 1)[:, :LANES][None]
    codes = id_codes(own_rows)
    for k in range(ranks):
        row_codes[k] = jnp.broadcast_to(codes[k : k + 1], (16, rows)).astype(BF16)
    img_t[...] = img_ref[...].T
    t_sum[...] = jnp.zeros_like(t_sum)

    pl.semaphore_wait(barrier, len(partners))

    cap_sends = iter(range(64))

    def send_caps(s, where):
        send(caps.at[s], caps.at[s], cap_send.at[next(cap_sends)], cap_recv.at[s], where)

    def caps_arrived(s):
        arrived(caps.at[s], cap_recv.at[s])

    mine = ids.at[pl.ds(wide, 1)]
    send(mine, mine, id_send.at[0], id_recv.at[0], at_wide(0, 0, 1))
    send_caps(wide, at_wide(0, near))
    send_caps(wide, at_wide(1, 0))
    send_caps(wide, at_wide(3, 0))
    send_caps(wide, at_wide(2, 0))
    send_caps(wide, at_wide(0, 2))
    send_caps(wide, at_wide(0, back))
    send_caps(wide, at_wide(0, 0, 1))

    def on_y(s):
        for dy in (1, 3, 2):
            send_caps(s, at_wide(dy, 0))

    def to_core(s):
        send_caps(s, at_wide(0, 0, 1))

    def targets(dy):
        base = 2 * NH * ((y + dy) % NY)
        turned = [id_codes(ids[base + i]).T[:own] for i in range(2 * NH)]
        select = lax.broadcasted_iota(jnp.int32, (8, ranks * LANES), 1) // LANES
        select = (select == lax.broadcasted_iota(jnp.int32, (8, ranks * LANES), 0)).astype(BF16)
        col_codes[...] = jnp.dot(
            jnp.concatenate(turned, axis=0).astype(BF16), select, preferred_element_type=F32
        ).astype(BF16)
        values = [jnp.full((16, 256), dw_ref[k], F32) for k in range(ranks + 1)]
        highs = [v.astype(BF16) for v in values]
        lows = [(v - w.astype(F32)).astype(BF16) for v, w in zip(values, highs)]
        size = 32

        def step(i, carry):
            for r in range(0, own, size):
                for c in range(0, rows, 256):
                    cut = slice(c, c + 256)
                    high = jnp.broadcast_to(highs[0][None], (size // 16, 16, 256))
                    rest = jnp.broadcast_to(lows[0][None], (size // 16, 16, 256))
                    for k in range(ranks):
                        col = col_codes[pl.ds(i * own + r, size), k * LANES : (k + 1) * LANES]
                        col = col.reshape(size // 16, 16, LANES)
                        same = jnp.concatenate([col, col], axis=2) == row_codes[k, :, cut][None]
                        high = jnp.where(same, highs[k + 1][None], high)
                        rest = jnp.where(same, lows[k + 1][None], rest)
                    t_high[base + i, pl.ds(r, size), cut] = high.reshape(size, 256)
                    t_low[base + i, pl.ds(r, size), cut] = rest.reshape(size, 256)
                    t_sum[:, cut] += jnp.sum(high.astype(F32) + rest.astype(F32), axis=0)
            return carry

        lax.fori_loop(0, 2 * NH, step, 0, unroll=4)

    def products(slots, biggest):
        for first, second in zip(slots[::2], slots[1::2]):
            block = jnp.concatenate([caps[first], caps[second]], axis=0)
            s = jnp.dot(block, img_t[...], preferred_element_type=F32)
            e_buf[first] = s[:own]
            e_buf[second] = s[own:]
            biggest = jnp.maximum(biggest, jnp.max(s.reshape(pair // 8, 8, rows), axis=0))
        return biggest

    def exponentials(slots, order, peak, biggest, total):
        new_peak = jnp.max(biggest, axis=0, keepdims=True)
        shrink = jnp.exp2((peak - new_peak) * to_exp2)
        part = jnp.zeros((8, rows), F32)
        for s in slots:
            e = jnp.exp2((e_buf[s] - new_peak) * to_exp2)
            e_buf[s] = e
            e_low[s] = e.astype(BF16)
            part = part + jnp.sum(e.reshape(own // 8, 8, rows), axis=0)
        peaks[order : order + 1] = new_peak
        return new_peak, shrink, total * shrink + jnp.sum(part, axis=0, keepdims=True)

    def moments(slots, shrink, first):
        turned = jnp.concatenate([caps[s] for s in slots], axis=0).T
        for j in range(0, rows, 256):
            cut = slice(j, j + 256)
            low_e = jnp.concatenate([e_low[s, :, cut] for s in slots], axis=0)
            high_t = jnp.concatenate([t_high[s, :, cut] for s in slots], axis=0)
            new_e = jnp.dot(turned, low_e, preferred_element_type=F32)
            new_t = jnp.dot(turned, high_t, preferred_element_type=F32)
            if first:
                acc_e[:, cut] = new_e
                acc_t[:, cut] = new_t
            else:
                acc_e[:, cut] = acc_e[:, cut] * shrink[:, cut] + new_e
                acc_t[:, cut] = acc_t[:, cut] + new_t

    arrived(ids.at[pl.ds(slot(0, 0, 1), 1)], id_recv.at[0])
    both = ids.at[pl.ds(2 * chip(0, 0), 2)]
    for d in range(1, NH):
        send(both, both, id_send.at[d], id_recv.at[NH - d], at_wide(0, d))

    caps_arrived(slot(0, back))
    on_y(slot(0, back))
    to_core(slot(0, back))
    for d in range(1, NH):
        arrived(ids.at[pl.ds(2 * chip(0, d), 2)], id_recv.at[d])
    column = ids.at[pl.ds(2 * NH * y, 2 * NH)]
    for d in range(1, NY):
        send(column, column, id_send.at[NH - 1 + d], id_recv.at[NH - 1 + NY - d], at_wide(d, 0))
    for dy in (1, 3, 2):
        caps_arrived(slot(dy, 0))
        send_caps(slot(dy, 0), at_wide(0, back))
        to_core(slot(dy, 0))
    targets(0)
    first = [slot(dy, 0, dc) for dy in range(NY) for dc in (0, 1)]
    for dy in range(NY):
        caps_arrived(slot(dy, 0, 1))
    peak = jnp.full((1, rows), -jnp.inf, F32)
    exp_total = jnp.zeros((1, rows), F32)
    biggest = products(first, jnp.broadcast_to(peak, (8, rows)))
    caps_arrived(slot(0, 2))
    on_y(slot(0, 2))
    to_core(slot(0, 2))
    peak, shrink, exp_total = exponentials(first, 0, peak, biggest, exp_total)
    caps_arrived(slot(0, near))
    to_core(slot(0, near))
    for dy in range(1, NY):
        arrived(ids.at[pl.ds(2 * NH * ((y + dy) % NY), 2 * NH)], id_recv.at[NH - 1 + dy])
        targets(dy)
    moments(first, shrink, True)
    for dy in (1, 3, 2):
        caps_arrived(slot(dy, back))
        to_core(slot(dy, back))
    for dh in (2, near, back):
        caps_arrived(slot(0, dh, 1))
    for dy in (1, 3, 2):
        caps_arrived(slot(dy, near, 1))
    second = [slot(0, dh, dc) for dh in (2, near, back) for dc in (0, 1)]
    for dy in (1, 3, 2):
        second += [slot(dy, back), slot(dy, near, 1)]
    biggest = products(second, jnp.broadcast_to(peak, (8, rows)))
    peak, shrink, exp_total = exponentials(second, 1, peak, biggest, exp_total)
    moments(second, shrink, False)
    for dy in (1, 3, 2):
        for dh in (2, near):
            caps_arrived(slot(dy, dh))
            to_core(slot(dy, dh))
    third = []
    biggest = jnp.broadcast_to(peak, (8, rows))
    for dy in (1, 3, 2):
        caps_arrived(slot(dy, 2, 1))
        caps_arrived(slot(dy, back, 1))
        more = [slot(dy, 2), slot(dy, 2, 1), slot(dy, near), slot(dy, back, 1)]
        biggest = products(more, biggest)
        third += more
    peak, shrink, exp_total = exponentials(third, 2, peak, biggest, exp_total)

    stat_out[...] = jnp.concatenate(
        [peak, exp_total, jnp.sum(t_sum[...], axis=0, keepdims=True), jnp.zeros((5, rows), F32)], axis=0
    )
    k = 0
    for dl in range(NL):
        for dx in range(NX):
            if dx or dl:
                theirs = ((NL - dl) % NL) * NX + (NX - dx) % NX
                send(stat_out, stat_in.at[theirs], stat_send.at[k], stat_recv.at[theirs], at_narrow(dx, dl))
                k += 1
    moments(third, shrink, False)
    for k in range(1, NL * NX):
        arrived(stat_in.at[k], stat_recv.at[k])
    stats = [stat_out[...]] + [stat_in[k] for k in range(1, NL * NX)]
    top = functools.reduce(jnp.maximum, [s[0:1] for s in stats])
    exp_all = sum(s[1:2] * jnp.exp2((s[0:1] - top) * to_exp2) for s in stats)
    t_all = sum(s[2:3] for s in stats)
    factor_e = sw_ref[...].reshape(1, rows) / exp_all
    factor_t = sw_ref[...].reshape(1, rows) / t_all
    to_e = [factor_e * jnp.exp2((peaks[i : i + 1] - top) * to_exp2) for i in range(3)]

    def group(dy, dh, c):
        if dh == 0:
            return 0
        if dy == 0:
            return 1
        if dh == 2:
            return 2
        return 1 if dh == 3 - 2 * c else 2

    def terms(dy, dh):
        g, k = chip(dy, dh), dy * NH + dh
        grads = []
        for c in (0, 1):
            s = 2 * g + c
            target = t_high[s].astype(F32) + t_low[s].astype(F32)
            grads.append((to_e[group(dy, dh, c)] * e_buf[s] - factor_t * target).astype(BF16))
        p_own[k] = scale * jnp.dot(jnp.concatenate(grads, axis=0), img_ref[...], preferred_element_type=F32)
        p_out[k] = p_own[k, pl.ds((1 - core) * own, own), :].astype(BF16)
        send(p_out.at[k], p_in.at[k], p_send.at[k], p_recv.at[k], at_wide(0, 0, 1))

    def chip_sum(dy, dh):
        k = dy * NH + dh
        arrived(p_in.at[k], p_recv.at[k])
        return p_own[k, pl.ds(core * own, own), :] + p_in[k].astype(F32)

    def over_y(dy, which):
        ya_out[which, dy] = chip_sum(dy, (2, near)[which]).astype(BF16)
        send(
            ya_out.at[which, dy], ya_in.at[which, NY - dy], ya_send.at[which, dy], ya_recv.at[which, NY - dy],
            at_wide(dy, 0),
        )

    def over_z(dy):
        zs_out[dy] = chip_sum(dy, back).astype(BF16)
        send(zs_out.at[dy], zs_in.at[dy], zs_send.at[dy], zs_recv.at[dy], at_wide(0, back))

    def last_y(dy):
        arrived(zs_in.at[dy], zs_recv.at[dy])
        yf_out[dy] = (chip_sum(dy, 0) + zs_in[dy].astype(F32)).astype(BF16)
        send(yf_out.at[dy], yf_in.at[NY - dy], yf_send.at[dy], yf_recv.at[NY - dy], at_wide(dy, 0))

    def last_z(which):
        dh = (2, near, back)[which]
        value = chip_sum(0, dh)
        if which < 2:
            for dy in range(1, NY):
                arrived(ya_in.at[which, dy], ya_recv.at[which, dy])
                value = value + ya_in[which, dy].astype(F32)
        zf_out[which] = value.astype(BF16)
        send(zf_out.at[which], zf_in.at[which], zf_send.at[which], zf_recv.at[which], at_wide(0, dh))

    def last():
        value = chip_sum(0, 0)
        for dy in range(1, NY):
            arrived(yf_in.at[dy], yf_recv.at[dy])
            value = value + yf_in[dy].astype(F32)
        for which in range(3):
            arrived(zf_in.at[which], zf_recv.at[which])
            value = value + zf_in[which].astype(F32)
        gc_ref[...] = value

    def image_terms():
        own_e = scale * factor_e * jnp.exp2((peak - top) * to_exp2)
        own_t = scale * factor_t
        turned = (acc_e[...] * own_e - acc_t[...] * own_t).T
        x_out[...] = turned.reshape(NL, NX, own, width).astype(BF16)
        for d in range(1, NX):
            to = (x + d) % NX
            send(x_out.at[:, to], x_in.at[NX - d], x_send.at[d], x_recv.at[NX - d], at_narrow(d, 0))

    def image_sum():
        for d in range(1, NX):
            arrived(x_in.at[d], x_recv.at[d])

        def total(which):
            value = x_out[which, x].astype(F32)
            for d in range(1, NX):
                value = value + x_in[d, which].astype(F32)
            return value

        l_out[...] = total(1 - low).astype(BF16)
        send(l_out, l_in, l_send.at[0], l_recv.at[0], at_narrow(0, 1))
        gi_ref[...] = total(low)

    def image_finish():
        arrived(l_in, l_recv.at[0])
        gi_ref[...] = gi_ref[...] + l_in[...].astype(F32)

    for step in ((1, 2), (3, 2), (2, 2), (1, 1), (1, 3)):
        terms(*step)
    over_y(1, 0)
    terms(3, 1)
    terms(3, 3)
    over_y(3, 0)
    over_y(2, 0)
    terms(2, 1)
    terms(2, 3)
    over_z(1)
    over_y(1, 1)
    image_terms()
    over_z(3)
    over_y(3, 1)
    over_z(2)
    over_y(2, 1)
    terms(0, 1)
    terms(0, 3)
    terms(0, 2)
    terms(1, 0)
    last_z(2)
    terms(3, 0)
    terms(2, 0)
    terms(0, 0)
    last_z(0)
    for dy in (1, 3, 2):
        last_y(dy)
    last_z(1)
    image_sum()
    image_finish()
    last()
    for copy in sent:
        copy.wait_send()


def body(images, captions, taxon_paths, sample_weight, depth_weight):
    rows, width = images.shape
    own = captions.shape[0]
    pair = 2 * own
    ranks = taxon_paths.shape[0]
    slots = 2 * NY * NH
    chips = NY * NH
    vmem = pl.BlockSpec(memory_space=pltpu.VMEM)
    dma = pltpu.SemaphoreType.DMA
    scratch = [
        pltpu.VMEM((slots, own, width), BF16),
        pltpu.VMEM((width, rows), BF16),
        pltpu.VMEM((slots, 8, LANES), jnp.int32),
        pltpu.VMEM((ranks, 16, rows), BF16),
        pltpu.VMEM((2 * NH * own, ranks * LANES), BF16),
        pltpu.VMEM((slots, own, rows), F32),
        pltpu.VMEM((slots, own, rows), BF16),
        pltpu.VMEM((slots, own, rows), BF16),
        pltpu.VMEM((slots, own, rows), BF16),
        pltpu.VMEM((width, rows), F32),
        pltpu.VMEM((width, rows), F32),
        pltpu.VMEM((16, rows), F32),
        pltpu.VMEM((8, rows), F32),
        pltpu.VMEM((8, rows), F32),
        pltpu.VMEM((NL * NX, 8, rows), F32),
        pltpu.VMEM((chips, pair, width), F32),
        pltpu.VMEM((chips, own, width), BF16),
        pltpu.VMEM((chips, own, width), BF16),
        pltpu.VMEM((2, NY, own, width), BF16),
        pltpu.VMEM((2, NY, own, width), BF16),
        pltpu.VMEM((NY, own, width), BF16),
        pltpu.VMEM((NY, own, width), BF16),
        pltpu.VMEM((NY, own, width), BF16),
        pltpu.VMEM((NY, own, width), BF16),
        pltpu.VMEM((3, own, width), BF16),
        pltpu.VMEM((3, own, width), BF16),
        pltpu.VMEM((NL, NX, own, width), BF16),
        pltpu.VMEM((NX, NL, own, width), BF16),
        pltpu.VMEM((own, width), BF16),
        pltpu.VMEM((own, width), BF16),
        dma((64,)), dma((slots,)), dma((8,)), dma((8,)), dma((8,)), dma((8,)),
        dma((chips,)), dma((chips,)), dma((2, NY)), dma((2, NY)), dma((NY,)), dma((NY,)),
        dma((NY,)), dma((NY,)), dma((3,)), dma((3,)),
        dma((NX,)), dma((NX,)), dma((1,)), dma((1,)),
    ]
    out = jax.ShapeDtypeStruct((own, width), F32)
    pairs = slots * own * rows
    return pl.pallas_call(
        kernel,
        out_shape=(out, out),
        in_specs=[vmem, vmem, vmem, vmem, pl.BlockSpec(memory_space=pltpu.SMEM)],
        out_specs=(vmem, vmem),
        scratch_shapes=scratch,
        compiler_params=pltpu.CompilerParams(
            collective_id=0, has_side_effects=True, vmem_limit_bytes=58 * 1024 * 1024
        ),
        cost_estimate=pl.CostEstimate(
            flops=8 * pairs * width, bytes_accessed=4 * rows * width, transcendentals=pairs
        ),
    )(images, captions, taxon_paths, sample_weight, depth_weight)


def solution(mesh):
    return jax.shard_map(
        body,
        mesh=mesh,
        in_specs=(P("wide", None), P(("wide", "narrow"), None), P(None, "wide"), P("wide"), P()),
        out_specs=(P(("wide", "narrow"), None), P(("wide", "narrow"), None)),
        check_vma=False,
    )
```

```python
import functools
import math

import jax
import jax.numpy as jnp
from jax import lax
from jax.experimental import pallas as pl
from jax.experimental.pallas import tpu as pltpu
from jax.sharding import PartitionSpec as P

BF16, F32 = jnp.bfloat16, jnp.float32
NY, NH, NX, NL = 4, 4, 4, 2
LANES = 128


def id_codes(ids):
    return ((ids & 127) + 128).astype(F32) * jnp.exp2((ids >> 7).astype(F32))


def kernel(
    img_hbm, cap_ref, tax_ref, sw_ref, dw_ref, o_ref,
    img_ref, caps, img_t, codes, row_codes, col_codes, e_buf, e_low, t_high, t_low, acc_e, acc_t, t_sum, peaks,
    sum_out, sum_in, stat_out, stat_in,
    p_own, p_out, p_in, ya_out, ya_in, zs_out, zs_in, yf_out, yf_in, zf_out, zf_in,
    x_out, x_in, l_out, l_in,
    img_sem, cap_send, cap_recv, id_send, id_recv, sum_send, sum_recv, stat_send, stat_recv,
    p_send, p_recv, ya_send, ya_recv, zs_send, zs_recv, yf_send, yf_recv, zf_send, zf_recv,
    x_send, x_recv, l_send, l_recv,
):
    rows, width = img_ref.shape
    own = cap_ref.shape[0]
    pair = 2 * own
    ranks = tax_ref.shape[0]
    scale = width ** -0.5
    to_exp2 = scale * math.log2(math.e)

    wide, narrow = lax.axis_index("wide"), lax.axis_index("narrow")
    core, h, y = wide % 2, (wide // 2) % NH, wide // (2 * NH)
    x, low = narrow % NX, narrow // NX
    near, back = 1 + 2 * core, 3 - 2 * core

    def chip(dy, dh):
        return ((y + dy) % NY) * NH + (h + dh) % NH

    def slot(dy, dh, dc=0):
        return chip(dy, dh) * 2 + (core + dc) % 2

    def at_wide(dy, dh, dc=0):
        return {"wide": slot(dy, dh, dc)}

    def at_narrow(dx, dl):
        return {"narrow": ((low + dl) % NL) * NX + (x + dx) % NX}

    img_copy = pltpu.make_async_copy(img_hbm, img_ref, img_sem.at[0])
    img_copy.start()

    barrier = pltpu.get_barrier_semaphore()
    partners = [at_wide(0, 0, 1)]
    partners += [at_wide(0, d) for d in range(1, NH)] + [at_wide(d, 0) for d in range(1, NY)]
    partners += [at_narrow(dx, dl) for dl in range(NL) for dx in range(NX) if dx or dl]
    for partner in partners:
        pl.semaphore_signal(barrier, inc=1, device_id=partner, device_id_type=pl.DeviceIdType.MESH)

    sent = []

    def send(src, dst, send_sem, recv_sem, where):
        copy = pltpu.make_async_remote_copy(
            src_ref=src, dst_ref=dst, send_sem=send_sem, recv_sem=recv_sem,
            device_id=where, device_id_type=pl.DeviceIdType.MESH,
        )
        copy.start()
        sent.append(copy)

    def arrived(dst, recv_sem):
        pltpu.make_async_copy(dst, dst, recv_sem).wait()

    pl.semaphore_wait(barrier, len(partners))

    cap_sends = iter(range(64))

    def send_caps(s, where, src=None):
        src = caps.at[s] if src is None else src
        send(src, caps.at[s], cap_send.at[next(cap_sends)], cap_recv.at[s], where)

    def caps_arrived(s):
        arrived(caps.at[s], cap_recv.at[s])

    for where in ((1, 0), (3, 0), (2, 0)):
        send_caps(wide, at_wide(*where), cap_ref)

    own_codes = id_codes(tax_ref[...])
    padded = jnp.concatenate([own_codes, jnp.zeros((8 - ranks, rows), F32)], axis=0)
    mine = pltpu.roll(padded, (rows - own * narrow) % rows, 1)[:, :LANES]
    codes[pl.ds(core, 1), pl.ds(chip(0, 0), 1)] = jnp.concatenate([mine, mine], axis=0).astype(BF16)[None, None]

    def code_part(c, first, count):
        return codes.at[c, pl.ds(first, count)]

    part = code_part(core, chip(0, 0), 1)
    for d in (1, 3, 2):
        send(part, part, id_send.at[d], id_recv.at[NH - d], at_wide(0, d))
    for where in ((0, 1), (0, 3), (0, 2), (0, 0, 1)):
        send_caps(wide, at_wide(*where), cap_ref)

    caps[pl.ds(wide, 1)] = cap_ref[...][None]
    for k in range(ranks):
        row_codes[k] = jnp.broadcast_to(own_codes[k : k + 1], (16, rows)).astype(BF16)
    t_sum[...] = jnp.zeros_like(t_sum)

    def on_y(s, places):
        for dy in places:
            send_caps(s, at_wide(dy, 0))

    def to_core(s):
        send_caps(s, at_wide(0, 0, 1))

    def targets(dy):
        first = NH * ((y + dy) % NY)
        tiles = [[codes[c, first + i].astype(F32)[:8] for c in (0, 1)] for i in range(NH)]
        turned = [jnp.concatenate(tile, axis=0).T[:own] for tile in tiles]
        shape = (16, 2 * ranks * LANES)
        column, row = (lax.broadcasted_iota(jnp.int32, shape, d) for d in (1, 0))
        block = column // LANES
        select = (row == block + jnp.where(block >= ranks, 8 - ranks, 0)).astype(BF16)
        col_codes[...] = jnp.dot(
            jnp.concatenate(turned, axis=0).astype(BF16), select, preferred_element_type=F32
        ).astype(BF16)
        values = [jnp.full((16, 256), dw_ref[k], F32) for k in range(ranks + 1)]
        highs = [v.astype(BF16) for v in values]
        lows = [(v - w.astype(F32)).astype(BF16) for v, w in zip(values, highs)]
        size = 32

        def step(i, carry):
            for c, j in ((c, j) for c in (0, 1) for j in range(0, rows, 256)):
                cut = slice(j, j + 256)
                small = []
                for r in range(0, own, size):
                    high = jnp.broadcast_to(highs[0][None], (size // 16, 16, 256))
                    rest = jnp.broadcast_to(lows[0][None], (size // 16, 16, 256))
                    for k in range(ranks):
                        lane = (c * ranks + k) * LANES
                        col = col_codes[pl.ds(i * own + r, size), lane : lane + LANES]
                        col = col.reshape(size // 16, 16, LANES)
                        same = jnp.concatenate([col, col], axis=2) == row_codes[k, :, cut][None]
                        high = jnp.where(same, highs[k + 1][None], high)
                        rest = jnp.where(same, lows[k + 1][None], rest)
                    t_high[2 * (first + i) + c, pl.ds(r, size), cut] = high.reshape(size, 256)
                    t_low[2 * (first + i) + c, pl.ds(r, size), cut] = rest.reshape(size, 256)
                    small += [rest[q] for q in range(size // 16)]
                while len(small) > 1:
                    small = [a + b for a, b in zip(small[::2], small[1::2])] + small[len(small) // 2 * 2 :]
                t_sum[:, cut] += small[0].astype(F32)
            return carry

        lax.fori_loop(0, NH, step, 0, unroll=2)
        ones = jnp.ones((16, 2 * NH * own), BF16)
        for j in range(0, rows, 256):
            cut = slice(j, j + 256)
            block = t_high[pl.ds(2 * first, 2 * NH), :, cut].reshape(2 * NH * own, 256)
            t_sum[:1, cut] += jnp.dot(ones, block, preferred_element_type=F32)[:1]

    def products(slots, biggest):
        for first, second in zip(slots[::2], slots[1::2]):
            block = jnp.concatenate([caps[first], caps[second]], axis=0)
            s = jnp.dot(block, img_t[...], preferred_element_type=F32)
            e_buf[first] = s[:own]
            e_buf[second] = s[own:]
            biggest = jnp.maximum(biggest, jnp.max(s.reshape(pair // 8, 8, rows), axis=0))
        return biggest

    def exponentials(slots, order, peak, biggest, total):
        new_peak = jnp.max(biggest, axis=0, keepdims=True)
        shrink = jnp.exp2((peak - new_peak) * to_exp2)
        part = jnp.zeros((8, rows), F32)
        for s in slots:
            e = jnp.exp2((e_buf[s] - new_peak) * to_exp2)
            e_buf[s] = e
            e_low[s] = e.astype(BF16)
            part = part + jnp.sum(e.reshape(own // 8, 8, rows), axis=0)
        peaks[order : order + 1] = new_peak
        return new_peak, shrink, total * shrink + jnp.sum(part, axis=0, keepdims=True)

    def moments(slots, shrink, first):
        turned = jnp.concatenate([caps[s] for s in slots], axis=0).T
        for j in range(0, rows, 256):
            cut = slice(j, j + 256)
            low_e = jnp.concatenate([e_low[s, :, cut] for s in slots], axis=0)
            high_t = jnp.concatenate([t_high[s, :, cut] for s in slots], axis=0)
            new_e = jnp.dot(turned, low_e, preferred_element_type=F32)
            new_t = jnp.dot(turned, high_t, preferred_element_type=F32)
            if first:
                acc_e[:, cut] = new_e
                acc_t[:, cut] = new_t
            else:
                acc_e[:, cut] = acc_e[:, cut] * shrink[:, cut] + new_e
                acc_t[:, cut] = acc_t[:, cut] + new_t

    def everyone():
        for dl in range(NL):
            for dx in range(NX):
                if dx or dl:
                    yield dl * NX + dx, ((NL - dl) % NL) * NX + (NX - dx) % NX, at_narrow(dx, dl)

    def folded(row):
        pieces = [row[:, j : j + LANES] for j in range(0, rows, LANES)]
        return jnp.concatenate(pieces + [jnp.zeros((8 - len(pieces), LANES), F32)], axis=0)

    def flat(tile):
        return jnp.concatenate([tile[i : i + 1] for i in range(rows // LANES)], axis=1)

    img_copy.wait()
    img_t[...] = img_ref[...].T

    for d in (1, 3, 2):
        arrived(code_part(core, chip(0, d), 1), id_recv.at[d])
    part = code_part(core, NH * y, NH)
    for d in (1, 3, 2):
        send(part, part, id_send.at[NH - 1 + d], id_recv.at[NH - 1 + NY - d], at_wide(d, 0))
    send(part, part, id_send.at[7], id_recv.at[7], at_wide(0, 0, 1))
    for dh in (1, 3):
        caps_arrived(slot(0, dh))
        on_y(slot(0, dh), (1, 3))
        to_core(slot(0, dh))
    arrived(code_part(1 - core, NH * y, NH), id_recv.at[7])
    for dy in (1, 3, 2):
        caps_arrived(slot(dy, 0))
        if dy == 2:
            send_caps(slot(dy, 0), at_wide(0, 1))
            send_caps(slot(dy, 0), at_wide(0, 3))
        to_core(slot(dy, 0))
    targets(0)
    for dy in (1, 3, 2):
        part = code_part(core, NH * ((y + dy) % NY), NH)
        arrived(part, id_recv.at[NH - 1 + dy])
        send(part, part, id_send.at[7 + dy], id_recv.at[7 + dy], at_wide(0, 0, 1))
    corners = [(dy, dh) for dh in (1, 3) for dy in (1, 3)]
    first = [slot(dy, 0, dc) for dy in range(NY) for dc in (0, 1)]
    caps_arrived(slot(0, 2))
    on_y(slot(0, 2), (2, 1, 3))
    to_core(slot(0, 2))
    for dy in range(NY):
        caps_arrived(slot(dy, 0, 1))
    peak = jnp.full((1, rows), -jnp.inf, F32)
    exp_total = jnp.zeros((1, rows), F32)
    biggest = products(first, jnp.broadcast_to(peak, (8, rows)))
    peak, shrink, exp_total = exponentials(first, 0, peak, biggest, exp_total)
    for dy in (1, 3, 2):
        arrived(code_part(1 - core, NH * ((y + dy) % NY), NH), id_recv.at[7 + dy])
        targets(dy)
        if dy == 1:
            for place in corners:
                caps_arrived(slot(*place))
                to_core(slot(*place))
    sum_out[...] = folded(jnp.sum(t_sum[...], axis=0, keepdims=True))
    for k, mirror, where in everyone():
        send(sum_out, sum_in.at[mirror], sum_send.at[k], sum_recv.at[mirror], where)
    places = [(0, 1), (0, 3), (0, 2)] + corners
    second = [slot(*place, dc) for place in places for dc in (0, 1)]
    for place in places:
        caps_arrived(slot(*place, 1))
    biggest = products(second, jnp.broadcast_to(peak, (8, rows)))
    peak, shrink, exp_total = exponentials(second, 1, peak, biggest, exp_total)
    shrinks = [shrink]
    places = [(2, 1), (2, 3), (2, 2), (1, 2), (3, 2)]
    for place in places:
        caps_arrived(slot(*place))
        to_core(slot(*place))
    third = [slot(*place, dc) for place in places for dc in (0, 1)]
    biggest = jnp.broadcast_to(peak, (8, rows))
    for place in places:
        caps_arrived(slot(*place, 1))
        biggest = products([slot(*place), slot(*place, 1)], biggest)
    peak, shrink, exp_total = exponentials(third, 2, peak, biggest, exp_total)
    shrinks.append(shrink)

    stat_out[...] = jnp.concatenate([folded(peak), folded(exp_total)], axis=0)
    for k, mirror, where in everyone():
        send(stat_out, stat_in.at[mirror], stat_send.at[k], stat_recv.at[mirror], where)
    moments(first, None, True)
    moments(second, shrinks[0], False)
    for k, _, _ in everyone():
        arrived(sum_in.at[k], sum_recv.at[k])
    t_all = flat(sum_out[...] + sum(sum_in[k] for k, _, _ in everyone()))
    weight = sw_ref[...].reshape(1, rows)
    factor_t = weight / t_all
    moments(third, shrinks[1], False)
    for k, _, _ in everyone():
        arrived(stat_in.at[k], stat_recv.at[k])
    stats = [stat_out[...]] + [stat_in[k] for k, _, _ in everyone()]
    top = functools.reduce(jnp.maximum, [s[:8] for s in stats])
    exp_all = flat(sum(s[8:] * jnp.exp2((s[:8] - top) * to_exp2) for s in stats))
    top = flat(top)
    factor_e = weight / exp_all
    to_e = [factor_e * jnp.exp2((peaks[i : i + 1] - top) * to_exp2) for i in range(3)]

    def group(dy, dh):
        if dh == 0:
            return 0
        return 2 if dy == 2 or (dh == 2 and dy) else 1

    def terms(dy, dh):
        g, k = chip(dy, dh), dy * NH + dh
        grads = []
        for c in (0, 1):
            s = 2 * g + c
            target = t_high[s].astype(F32) + t_low[s].astype(F32)
            grads.append((to_e[group(dy, dh)] * e_buf[s] - factor_t * target).astype(BF16))
        p_own[k] = scale * jnp.dot(jnp.concatenate(grads, axis=0), img_ref[...], preferred_element_type=F32)
        p_out[k] = p_own[k, pl.ds((1 - core) * own, own), :].astype(BF16)
        send(p_out.at[k], p_in.at[k], p_send.at[k], p_recv.at[k], at_wide(0, 0, 1))

    def chip_sum(dy, dh):
        k = dy * NH + dh
        arrived(p_in.at[k], p_recv.at[k])
        return p_own[k, pl.ds(core * own, own), :] + p_in[k].astype(F32)

    def over_y(dy, which):
        ya_out[which, dy] = chip_sum(dy, (2, near)[which]).astype(BF16)
        send(
            ya_out.at[which, dy], ya_in.at[which, NY - dy], ya_send.at[which, dy], ya_recv.at[which, NY - dy],
            at_wide(dy, 0),
        )

    def over_z(dy):
        zs_out[dy] = chip_sum(dy, back).astype(BF16)
        send(zs_out.at[dy], zs_in.at[dy], zs_send.at[dy], zs_recv.at[dy], at_wide(0, back))

    def last_y(dy):
        arrived(zs_in.at[dy], zs_recv.at[dy])
        yf_out[dy] = (chip_sum(dy, 0) + zs_in[dy].astype(F32)).astype(BF16)
        send(yf_out.at[dy], yf_in.at[NY - dy], yf_send.at[dy], yf_recv.at[NY - dy], at_wide(dy, 0))

    def last_z(which):
        dh = (2, near, back)[which]
        value = chip_sum(0, dh)
        if which < 2:
            for dy in range(1, NY):
                arrived(ya_in.at[which, dy], ya_recv.at[which, dy])
                value = value + ya_in[which, dy].astype(F32)
        zf_out[which] = value.astype(BF16)
        send(zf_out.at[which], zf_in.at[which], zf_send.at[which], zf_recv.at[which], at_wide(0, dh))

    def last():
        value = chip_sum(0, 0)
        for dy in range(1, NY):
            arrived(yf_in.at[dy], yf_recv.at[dy])
            value = value + yf_in[dy].astype(F32)
        for which in range(3):
            arrived(zf_in.at[which], zf_recv.at[which])
            value = value + zf_in[which].astype(F32)
        o_ref[1] = value

    def image_terms():
        own_e = scale * factor_e * jnp.exp2((peak - top) * to_exp2)
        own_t = scale * factor_t
        turned = (acc_e[...] * own_e - acc_t[...] * own_t).T
        x_out[...] = turned.reshape(NL, NX, own, width).astype(BF16)
        for d in range(1, NX):
            to = (x + d) % NX
            send(x_out.at[:, to], x_in.at[NX - d], x_send.at[d], x_recv.at[NX - d], at_narrow(d, 0))

    def image_sum():
        for d in range(1, NX):
            arrived(x_in.at[d], x_recv.at[d])

        def total(which):
            value = x_out[which, x].astype(F32)
            for d in range(1, NX):
                value = value + x_in[d, which].astype(F32)
            return value

        l_out[...] = total(1 - low).astype(BF16)
        send(l_out, l_in, l_send.at[0], l_recv.at[0], at_narrow(0, 1))
        o_ref[0] = total(low)

    def image_finish():
        arrived(l_in, l_recv.at[0])
        o_ref[0] = o_ref[0] + l_in[...].astype(F32)

    for step in ((1, 2), (3, 2), (2, 2), (1, 1), (1, 3)):
        terms(*step)
    over_y(1, 0)
    terms(3, 1)
    terms(3, 3)
    over_y(3, 0)
    over_y(2, 0)
    terms(2, 1)
    terms(2, 3)
    over_z(1)
    over_y(1, 1)
    image_terms()
    over_z(3)
    over_y(3, 1)
    over_z(2)
    over_y(2, 1)
    terms(0, 1)
    terms(0, 3)
    terms(0, 2)
    terms(1, 0)
    last_z(2)
    terms(3, 0)
    terms(2, 0)
    terms(0, 0)
    last_z(0)
    for dy in (1, 3, 2):
        last_y(dy)
    last_z(1)
    image_sum()
    image_finish()
    last()
    for copy in sent:
        copy.wait_send()


def body(images, captions, taxon_paths, sample_weight, depth_weight):
    rows, width = images.shape
    own = captions.shape[0]
    pair = 2 * own
    ranks = taxon_paths.shape[0]
    slots = 2 * NY * NH
    chips = NY * NH
    vmem = pl.BlockSpec(memory_space=pltpu.VMEM)
    dma = pltpu.SemaphoreType.DMA
    scratch = [
        pltpu.VMEM((rows, width), BF16),
        pltpu.VMEM((slots, own, width), BF16),
        pltpu.VMEM((width, rows), BF16),
        pltpu.VMEM((2, chips, 16, LANES), BF16),
        pltpu.VMEM((ranks, 16, rows), BF16),
        pltpu.VMEM((NH * own, 2 * ranks * LANES), BF16),
        pltpu.VMEM((slots, own, rows), F32),
        pltpu.VMEM((slots, own, rows), BF16),
        pltpu.VMEM((slots, own, rows), BF16),
        pltpu.VMEM((slots, own, rows), BF16),
        pltpu.VMEM((width, rows), F32),
        pltpu.VMEM((width, rows), F32),
        pltpu.VMEM((16, rows), F32),
        pltpu.VMEM((8, rows), F32),
        pltpu.VMEM((8, LANES), F32),
        pltpu.VMEM((NL * NX, 8, LANES), F32),
        pltpu.VMEM((16, LANES), F32),
        pltpu.VMEM((NL * NX, 16, LANES), F32),
        pltpu.VMEM((chips, pair, width), F32),
        pltpu.VMEM((chips, own, width), BF16),
        pltpu.VMEM((chips, own, width), BF16),
        pltpu.VMEM((2, NY, own, width), BF16),
        pltpu.VMEM((2, NY, own, width), BF16),
        pltpu.VMEM((NY, own, width), BF16),
        pltpu.VMEM((NY, own, width), BF16),
        pltpu.VMEM((NY, own, width), BF16),
        pltpu.VMEM((NY, own, width), BF16),
        pltpu.VMEM((3, own, width), BF16),
        pltpu.VMEM((3, own, width), BF16),
        pltpu.VMEM((NL, NX, own, width), BF16),
        pltpu.VMEM((NX, NL, own, width), BF16),
        pltpu.VMEM((own, width), BF16),
        pltpu.VMEM((own, width), BF16),
        dma((1,)), dma((64,)), dma((slots,)), dma((12,)), dma((12,)), dma((8,)), dma((8,)), dma((8,)), dma((8,)),
        dma((chips,)), dma((chips,)), dma((2, NY)), dma((2, NY)), dma((NY,)), dma((NY,)),
        dma((NY,)), dma((NY,)), dma((3,)), dma((3,)),
        dma((NX,)), dma((NX,)), dma((1,)), dma((1,)),
    ]
    out = jax.ShapeDtypeStruct((2, own, width), F32)
    pairs = slots * own * rows
    o = pl.pallas_call(
        kernel,
        out_shape=out,
        in_specs=[pl.BlockSpec(memory_space=pl.ANY), vmem, vmem, vmem, pl.BlockSpec(memory_space=pltpu.SMEM)],
        out_specs=vmem,
        scratch_shapes=scratch,
        compiler_params=pltpu.CompilerParams(
            collective_id=0, has_side_effects=True, vmem_limit_bytes=58 * 1024 * 1024
        ),
        cost_estimate=pl.CostEstimate(
            flops=8 * pairs * width, bytes_accessed=4 * rows * width, transcendentals=pairs
        ),
    )(images, captions, taxon_paths, sample_weight, depth_weight)
    return o[0], o[1]


def solution(mesh):
    return jax.shard_map(
        body,
        mesh=mesh,
        in_specs=(P("wide", None), P(("wide", "narrow"), None), P(None, "wide"), P("wide"), P()),
        out_specs=(P(("wide", "narrow"), None), P(("wide", "narrow"), None)),
        check_vma=False,
    )
```

```python
import functools
import math

import jax
import jax.numpy as jnp
from jax import lax
from jax.experimental import pallas as pl
from jax.experimental.pallas import tpu as pltpu
from jax.sharding import PartitionSpec as P

BF16, F32 = jnp.bfloat16, jnp.float32
NY, NH, NX, NL = 4, 4, 4, 2
LANES = 128


def id_codes(ids):
    return ((ids & 127) + 128).astype(F32) * jnp.exp2((ids >> 7).astype(F32))


def kernel(
    img_hbm, cap_ref, tax_ref, sw_ref, dw_ref, o_ref,
    img_ref, caps, img_t, codes, select, row_codes, col_codes, e_buf, e_low, t_high, t_low, acc_e, acc_t, t_sum, peaks,
    sum_out, sum_in, stat_out, stat_in,
    p_own, p_out, p_in, ya_out, ya_in, zs_out, zs_in, yf_out, yf_in, zf_out, zf_in,
    x_out, x_in, l_out, l_in,
    img_sem, cap_send, cap_recv, id_send, id_recv, sum_send, sum_recv, stat_send, stat_recv,
    p_send, p_recv, ya_send, ya_recv, zs_send, zs_recv, yf_send, yf_recv, zf_send, zf_recv,
    x_send, x_recv, l_send, l_recv,
):
    rows, width = img_ref.shape
    own = cap_ref.shape[0]
    pair = 2 * own
    ranks = tax_ref.shape[0]
    scale = width ** -0.5
    to_exp2 = scale * math.log2(math.e)

    wide, narrow = lax.axis_index("wide"), lax.axis_index("narrow")
    core, h, y = wide % 2, (wide // 2) % NH, wide // (2 * NH)
    x, low = narrow % NX, narrow // NX
    def chip(dy, dh):
        return ((y + dy) % NY) * NH + (h + dh) % NH

    def slot(dy, dh, dc=0):
        return chip(dy, dh) * 2 + (core + dc) % 2

    def at_wide(dy, dh, dc=0):
        return {"wide": slot(dy, dh, dc)}

    def at_narrow(dx, dl):
        return {"narrow": ((low + dl) % NL) * NX + (x + dx) % NX}

    img_copy = pltpu.make_async_copy(img_hbm, img_ref, img_sem.at[0])
    img_copy.start()

    barrier = pltpu.get_barrier_semaphore()
    partners = [at_wide(0, 0, 1)]
    partners += [at_wide(0, d) for d in range(1, NH)] + [at_wide(d, 0) for d in range(1, NY)]
    partners += [at_narrow(dx, dl) for dl in range(NL) for dx in range(NX) if dx or dl]
    for partner in partners:
        pl.semaphore_signal(barrier, inc=1, device_id=partner, device_id_type=pl.DeviceIdType.MESH)

    sent = []

    def send(src, dst, send_sem, recv_sem, where):
        copy = pltpu.make_async_remote_copy(
            src_ref=src, dst_ref=dst, send_sem=send_sem, recv_sem=recv_sem,
            device_id=where, device_id_type=pl.DeviceIdType.MESH,
        )
        copy.start()
        sent.append(copy)

    def arrived(dst, recv_sem):
        pltpu.make_async_copy(dst, dst, recv_sem).wait()

    pl.semaphore_wait(barrier, len(partners))

    cap_sends = iter(range(64))

    def send_caps(s, where, src=None):
        src = caps.at[s] if src is None else src
        send(src, caps.at[s], cap_send.at[next(cap_sends)], cap_recv.at[s], where)

    def caps_arrived(s):
        arrived(caps.at[s], cap_recv.at[s])

    for where in ((1, 0), (3, 0), (2, 0)):
        send_caps(wide, at_wide(*where), cap_ref)

    own_codes = id_codes(tax_ref[...])
    padded = jnp.concatenate([own_codes, jnp.zeros((8 - ranks, rows), F32)], axis=0)
    mine = pltpu.roll(padded, (rows - own * narrow) % rows, 1)[:, :LANES]
    codes[pl.ds(core, 1), pl.ds(chip(0, 0), 1)] = jnp.concatenate([mine, mine], axis=0).astype(BF16)[None, None]

    def code_part(c, first, count):
        return codes.at[c, pl.ds(first, count)]

    part = code_part(core, chip(0, 0), 1)
    for d in (1, 3, 2):
        send(part, part, id_send.at[d], id_recv.at[NH - d], at_wide(0, d))
    for where in ((0, 1), (0, 3), (0, 2), (0, 0, 1)):
        send_caps(wide, at_wide(*where), cap_ref)

    caps[pl.ds(wide, 1)] = cap_ref[...][None]
    for k in range(ranks):
        row_codes[k] = jnp.broadcast_to(own_codes[k : k + 1], (16, rows)).astype(BF16)
    t_sum[...] = jnp.zeros_like(t_sum)

    def on_y(s, places):
        for dy in places:
            send_caps(s, at_wide(dy, 0))

    def to_core(s):
        send_caps(s, at_wide(0, 0, 1))

    def targets(dy, beside=()):
        first = NH * ((y + dy) % NY)
        tiles = [[codes[c, first + i].astype(F32)[:8] for c in (0, 1)] for i in range(NH)]
        turned = [jnp.concatenate(tile, axis=0).T[:own] for tile in tiles]
        col_codes[...] = jnp.dot(
            jnp.concatenate(turned, axis=0).astype(BF16), select[...], preferred_element_type=F32
        ).astype(BF16)
        values = [jnp.full((16, 256), dw_ref[k], F32) for k in range(ranks + 1)]
        highs = [v.astype(BF16) for v in values]
        lows = [(v - w.astype(F32)).astype(BF16) for v, w in zip(values, highs)]
        size = 32

        def step(i):
            for c, j in ((c, j) for c in (0, 1) for j in range(0, rows, 256)):
                cut = slice(j, j + 256)
                small = []
                for r in range(0, own, size):
                    high = jnp.broadcast_to(highs[0][None], (size // 16, 16, 256))
                    rest = jnp.broadcast_to(lows[0][None], (size // 16, 16, 256))
                    for k in range(ranks):
                        lane = (c * ranks + k) * LANES
                        col = col_codes[pl.ds(i * own + r, size), lane : lane + LANES]
                        col = col.reshape(size // 16, 16, LANES)
                        same = jnp.concatenate([col, col], axis=2) == row_codes[k, :, cut][None]
                        high = jnp.where(same, highs[k + 1][None], high)
                        rest = jnp.where(same, lows[k + 1][None], rest)
                    t_high[2 * (first + i) + c, pl.ds(r, size), cut] = high.reshape(size, 256)
                    t_low[2 * (first + i) + c, pl.ds(r, size), cut] = rest.reshape(size, 256)
                    small += [rest[q] for q in range(size // 16)]
                while len(small) > 1:
                    small = [a + b for a, b in zip(small[::2], small[1::2])] + small[len(small) // 2 * 2 :]
                t_sum[:, cut] += small[0].astype(F32)

        for i in range(NH):
            step(i)
            if i < len(beside):
                beside[i]()
        ones = jnp.ones((16, 2 * NH * own), BF16)
        for j in range(0, rows, 256):
            cut = slice(j, j + 256)
            block = t_high[pl.ds(2 * first, 2 * NH), :, cut].reshape(2 * NH * own, 256)
            t_sum[:1, cut] += jnp.dot(ones, block, preferred_element_type=F32)[:1]

    def products(slots, biggest):
        for first, second in zip(slots[::2], slots[1::2]):
            block = jnp.concatenate([caps[first], caps[second]], axis=0)
            s = jnp.dot(block, img_t[...], preferred_element_type=F32)
            e_buf[first] = s[:own]
            e_buf[second] = s[own:]
            biggest = jnp.maximum(biggest, jnp.max(s.reshape(pair // 8, 8, rows), axis=0))
        return biggest

    def exponentials(slots, order, peak, biggest, total):
        new_peak = jnp.max(biggest, axis=0, keepdims=True)
        shrink = jnp.exp2((peak - new_peak) * to_exp2)
        part = jnp.zeros((8, rows), F32)
        for s in slots:
            e = jnp.exp2((e_buf[s] - new_peak) * to_exp2)
            e_buf[s] = e
            e_low[s] = e.astype(BF16)
            part = part + jnp.sum(e.reshape(own // 8, 8, rows), axis=0)
        peaks[order : order + 1] = new_peak
        return new_peak, shrink, total * shrink + jnp.sum(part, axis=0, keepdims=True)

    def moments(slots, shrink, first):
        turned = jnp.concatenate([caps[s] for s in slots], axis=0).T
        for j in range(0, rows, 256):
            cut = slice(j, j + 256)
            low_e = jnp.concatenate([e_low[s, :, cut] for s in slots], axis=0)
            high_t = jnp.concatenate([t_high[s, :, cut] for s in slots], axis=0)
            new_e = jnp.dot(turned, low_e, preferred_element_type=F32)
            new_t = jnp.dot(turned, high_t, preferred_element_type=F32)
            if first:
                acc_e[:, cut] = new_e
                acc_t[:, cut] = new_t
            else:
                acc_e[:, cut] = acc_e[:, cut] * shrink[:, cut] + new_e
                acc_t[:, cut] = acc_t[:, cut] + new_t

    def everyone():
        for dl in range(NL):
            for dx in range(NX):
                if dx or dl:
                    yield dl * NX + dx, ((NL - dl) % NL) * NX + (NX - dx) % NX, at_narrow(dx, dl)

    def folded(row):
        pieces = [row[:, j : j + LANES] for j in range(0, rows, LANES)]
        return jnp.concatenate(pieces + [jnp.zeros((8 - len(pieces), LANES), F32)], axis=0)

    def flat(tile):
        return jnp.concatenate([tile[i : i + 1] for i in range(rows // LANES)], axis=1)

    shape = (16, 2 * ranks * LANES)
    column, row = (lax.broadcasted_iota(jnp.int32, shape, d) for d in (1, 0))
    block = column // LANES
    select[...] = (row == block + jnp.where(block >= ranks, 8 - ranks, 0)).astype(BF16)
    img_copy.wait()
    img_t[...] = img_ref[...].T

    for d in (1, 3, 2):
        arrived(code_part(core, chip(0, d), 1), id_recv.at[d])
    part = code_part(core, NH * y, NH)
    for d in (1, 3, 2):
        send(part, part, id_send.at[NH - 1 + d], id_recv.at[NH - 1 + NY - d], at_wide(d, 0))
    send(part, part, id_send.at[7], id_recv.at[7], at_wide(0, 0, 1))
    for dh in (1, 3):
        caps_arrived(slot(0, dh))
        on_y(slot(0, dh), (1, 3))
        to_core(slot(0, dh))
    arrived(code_part(1 - core, NH * y, NH), id_recv.at[7])
    for dy in (1, 3, 2):
        caps_arrived(slot(dy, 0))
        if dy == 2:
            send_caps(slot(dy, 0), at_wide(0, 1))
            send_caps(slot(dy, 0), at_wide(0, 3))
        to_core(slot(dy, 0))
    targets(0)
    for dy in (1, 3, 2):
        part = code_part(core, NH * ((y + dy) % NY), NH)
        arrived(part, id_recv.at[NH - 1 + dy])
        send(part, part, id_send.at[7 + dy], id_recv.at[7 + dy], at_wide(0, 0, 1))
    corners = [(dy, dh) for dh in (1, 3) for dy in (1, 3)]
    first = [slot(dy, 0, dc) for dy in range(NY) for dc in (0, 1)]
    caps_arrived(slot(0, 2))
    on_y(slot(0, 2), (2, 1, 3))
    to_core(slot(0, 2))
    for dy in range(NY):
        caps_arrived(slot(dy, 0, 1))
    peak = jnp.full((1, rows), -jnp.inf, F32)
    exp_total = jnp.zeros((1, rows), F32)
    largest = [jnp.broadcast_to(peak, (8, rows))]

    def pairs(slots):
        def product(two):
            largest[0] = products(two, largest[0])

        return [functools.partial(product, slots[i : i + 2]) for i in range(0, len(slots), 2)]

    def code_arrived(dy):
        arrived(code_part(1 - core, NH * ((y + dy) % NY), NH), id_recv.at[7 + dy])

    code_arrived(1)
    targets(1, pairs(first))
    peak, shrink, exp_total = exponentials(first, 0, peak, largest[0], exp_total)
    for place in corners:
        caps_arrived(slot(*place))
        to_core(slot(*place))
    column = [(0, 1), (0, 3), (0, 2)]
    second = [slot(*place, dc) for place in column + corners for dc in (0, 1)]
    for place in column:
        caps_arrived(slot(*place, 1))
    largest[0] = jnp.broadcast_to(peak, (8, rows))
    code_arrived(3)
    targets(3, pairs(second[:6]))
    code_arrived(2)
    late = [(2, 1), (2, 3), (2, 2), (1, 2), (3, 2)]
    for place in corners:
        caps_arrived(slot(*place, 1))
    targets(2, pairs(second[6:]))
    for place in late[:2]:
        caps_arrived(slot(*place))
        to_core(slot(*place))
    sum_out[...] = folded(jnp.sum(t_sum[...], axis=0, keepdims=True))
    for k, mirror, where in everyone():
        send(sum_out, sum_in.at[mirror], sum_send.at[k], sum_recv.at[mirror], where)
    for place in late[2:]:
        caps_arrived(slot(*place))
        to_core(slot(*place))
    peak, shrink, exp_total = exponentials(second, 1, peak, largest[0], exp_total)
    shrinks = [shrink]
    third = [slot(*place, dc) for place in late for dc in (0, 1)]
    biggest = jnp.broadcast_to(peak, (8, rows))
    for place in late:
        caps_arrived(slot(*place, 1))
        biggest = products([slot(*place), slot(*place, 1)], biggest)
    peak, shrink, exp_total = exponentials(third, 2, peak, biggest, exp_total)
    shrinks.append(shrink)

    stat_out[...] = jnp.concatenate([folded(peak), folded(exp_total)], axis=0)
    for k, mirror, where in everyone():
        send(stat_out, stat_in.at[mirror], stat_send.at[k], stat_recv.at[mirror], where)
    moments(first, None, True)
    moments(second, shrinks[0], False)
    for k, _, _ in everyone():
        arrived(sum_in.at[k], sum_recv.at[k])
    t_all = flat(sum_out[...] + sum(sum_in[k] for k, _, _ in everyone()))
    weight = sw_ref[...].reshape(1, rows)
    factor_t = weight / t_all
    moments(third, shrinks[1], False)
    for k, _, _ in everyone():
        arrived(stat_in.at[k], stat_recv.at[k])
    stats = [stat_out[...]] + [stat_in[k] for k, _, _ in everyone()]
    top = functools.reduce(jnp.maximum, [s[:8] for s in stats])
    exp_all = flat(sum(s[8:] * jnp.exp2((s[:8] - top) * to_exp2) for s in stats))
    top = flat(top)
    factor_e = weight / exp_all
    to_e = [factor_e * jnp.exp2((peaks[i : i + 1] - top) * to_exp2) for i in range(3)]

    def group(dy, dh):
        if dh == 0:
            return 0
        return 2 if dy == 2 or (dh == 2 and dy) else 1

    def terms(dy, dh):
        g, k = chip(dy, dh), dy * NH + dh
        grads = []
        for c in (0, 1):
            s = 2 * g + c
            target = t_high[s].astype(F32) + t_low[s].astype(F32)
            grads.append((to_e[group(dy, dh)] * e_buf[s] - factor_t * target).astype(BF16))
        p_own[k] = scale * jnp.dot(jnp.concatenate(grads, axis=0), img_ref[...], preferred_element_type=F32)
        p_out[k] = p_own[k, pl.ds((1 - core) * own, own), :].astype(BF16)
        send(p_out.at[k], p_in.at[k], p_send.at[k], p_recv.at[k], at_wide(0, 0, 1))

    def chip_sum(dy, dh):
        k = dy * NH + dh
        arrived(p_in.at[k], p_recv.at[k])
        return p_own[k, pl.ds(core * own, own), :] + p_in[k].astype(F32)

    def over_y(dy, dh):
        ya_out[dy, dh] = chip_sum(dy, dh).astype(BF16)
        send(
            ya_out.at[dy, dh], ya_in.at[NY - dy, dh], ya_send.at[dy, dh], ya_recv.at[NY - dy, dh], at_wide(dy, 0)
        )

    def over_z(dh):
        zs_out[dh] = chip_sum(2, dh).astype(BF16)
        send(zs_out.at[dh], zs_in.at[NH - dh], zs_send.at[dh], zs_recv.at[NH - dh], at_wide(0, dh))

    def last_y(dy):
        value = chip_sum(dy, 0)
        if dy == 2:
            for dh in (1, 3):
                arrived(zs_in.at[dh], zs_recv.at[dh])
                value = value + zs_in[dh].astype(F32)
        yf_out[dy] = value.astype(BF16)
        send(yf_out.at[dy], yf_in.at[NY - dy], yf_send.at[dy], yf_recv.at[NY - dy], at_wide(dy, 0))

    def last_z(dh):
        value = chip_sum(0, dh)
        for dy in (1, 3, 2) if dh == 2 else (1, 3):
            arrived(ya_in.at[dy, dh], ya_recv.at[dy, dh])
            value = value + ya_in[dy, dh].astype(F32)
        zf_out[dh] = value.astype(BF16)
        send(zf_out.at[dh], zf_in.at[NH - dh], zf_send.at[dh], zf_recv.at[NH - dh], at_wide(0, dh))

    def last():
        value = chip_sum(0, 0)
        for dy in range(1, NY):
            arrived(yf_in.at[dy], yf_recv.at[dy])
            value = value + yf_in[dy].astype(F32)
        for dh in range(1, NH):
            arrived(zf_in.at[dh], zf_recv.at[dh])
            value = value + zf_in[dh].astype(F32)
        o_ref[1] = value

    def image_terms():
        own_e = scale * factor_e * jnp.exp2((peak - top) * to_exp2)
        own_t = scale * factor_t
        turned = (acc_e[...] * own_e - acc_t[...] * own_t).T
        x_out[...] = turned.reshape(NL, NX, own, width).astype(BF16)
        for d in range(1, NX):
            to = (x + d) % NX
            send(x_out.at[:, to], x_in.at[NX - d], x_send.at[d], x_recv.at[NX - d], at_narrow(d, 0))

    def image_sum():
        for d in range(1, NX):
            arrived(x_in.at[d], x_recv.at[d])

        def total(which):
            value = x_out[which, x].astype(F32)
            for d in range(1, NX):
                value = value + x_in[d, which].astype(F32)
            return value

        l_out[...] = total(1 - low).astype(BF16)
        send(l_out, l_in, l_send.at[0], l_recv.at[0], at_narrow(0, 1))
        o_ref[0] = total(low)

    def image_finish():
        arrived(l_in, l_recv.at[0])
        o_ref[0] = o_ref[0] + l_in[...].astype(F32)

    for step in ((2, 1), (2, 3), (1, 2), (3, 2), (2, 2)):
        terms(*step)
    over_z(1)
    over_z(3)
    terms(1, 1)
    terms(3, 1)
    for dy in (1, 3, 2):
        over_y(dy, 2)
    terms(1, 3)
    terms(3, 3)
    over_y(1, 1)
    over_y(3, 1)
    image_terms()
    over_y(1, 3)
    over_y(3, 3)
    for step in ((1, 0), (3, 0), (2, 0), (0, 2), (0, 1)):
        terms(*step)
    last_y(1)
    last_y(3)
    terms(0, 3)
    terms(0, 0)
    last_z(2)
    last_y(2)
    last_z(1)
    last_z(3)
    image_sum()
    image_finish()
    last()
    for copy in sent:
        copy.wait_send()


def body(images, captions, taxon_paths, sample_weight, depth_weight):
    rows, width = images.shape
    own = captions.shape[0]
    pair = 2 * own
    ranks = taxon_paths.shape[0]
    slots = 2 * NY * NH
    chips = NY * NH
    vmem = pl.BlockSpec(memory_space=pltpu.VMEM)
    dma = pltpu.SemaphoreType.DMA
    scratch = [
        pltpu.VMEM((rows, width), BF16),
        pltpu.VMEM((slots, own, width), BF16),
        pltpu.VMEM((width, rows), BF16),
        pltpu.VMEM((2, chips, 16, LANES), BF16),
        pltpu.VMEM((16, 2 * ranks * LANES), BF16),
        pltpu.VMEM((ranks, 16, rows), BF16),
        pltpu.VMEM((NH * own, 2 * ranks * LANES), BF16),
        pltpu.VMEM((slots, own, rows), F32),
        pltpu.VMEM((slots, own, rows), BF16),
        pltpu.VMEM((slots, own, rows), BF16),
        pltpu.VMEM((slots, own, rows), BF16),
        pltpu.VMEM((width, rows), F32),
        pltpu.VMEM((width, rows), F32),
        pltpu.VMEM((16, rows), F32),
        pltpu.VMEM((8, rows), F32),
        pltpu.VMEM((8, LANES), F32),
        pltpu.VMEM((NL * NX, 8, LANES), F32),
        pltpu.VMEM((16, LANES), F32),
        pltpu.VMEM((NL * NX, 16, LANES), F32),
        pltpu.VMEM((chips, pair, width), F32),
        pltpu.VMEM((chips, own, width), BF16),
        pltpu.VMEM((chips, own, width), BF16),
        pltpu.VMEM((NY, NH, own, width), BF16),
        pltpu.VMEM((NY, NH, own, width), BF16),
        pltpu.VMEM((NH, own, width), BF16),
        pltpu.VMEM((NH, own, width), BF16),
        pltpu.VMEM((NY, own, width), BF16),
        pltpu.VMEM((NY, own, width), BF16),
        pltpu.VMEM((NH, own, width), BF16),
        pltpu.VMEM((NH, own, width), BF16),
        pltpu.VMEM((NL, NX, own, width), BF16),
        pltpu.VMEM((NX, NL, own, width), BF16),
        pltpu.VMEM((own, width), BF16),
        pltpu.VMEM((own, width), BF16),
        dma((1,)), dma((64,)), dma((slots,)), dma((12,)), dma((12,)), dma((8,)), dma((8,)), dma((8,)), dma((8,)),
        dma((chips,)), dma((chips,)), dma((NY, NH)), dma((NY, NH)), dma((NH,)), dma((NH,)),
        dma((NY,)), dma((NY,)), dma((NH,)), dma((NH,)),
        dma((NX,)), dma((NX,)), dma((1,)), dma((1,)),
    ]
    out = jax.ShapeDtypeStruct((2, own, width), F32)
    pairs = slots * own * rows
    o = pl.pallas_call(
        kernel,
        out_shape=out,
        in_specs=[pl.BlockSpec(memory_space=pl.ANY), vmem, vmem, vmem, pl.BlockSpec(memory_space=pltpu.SMEM)],
        out_specs=vmem,
        scratch_shapes=scratch,
        compiler_params=pltpu.CompilerParams(
            collective_id=0, has_side_effects=True, vmem_limit_bytes=58 * 1024 * 1024
        ),
        cost_estimate=pl.CostEstimate(
            flops=8 * pairs * width, bytes_accessed=4 * rows * width, transcendentals=pairs
        ),
    )(images, captions, taxon_paths, sample_weight, depth_weight)
    return o[0], o[1]


def solution(mesh):
    return jax.shard_map(
        body,
        mesh=mesh,
        in_specs=(P("wide", None), P(("wide", "narrow"), None), P(None, "wide"), P("wide"), P()),
        out_specs=(P(("wide", "narrow"), None), P(("wide", "narrow"), None)),
        check_vma=False,
    )
```

```python
import functools
import math

import jax
import jax.numpy as jnp
from jax import lax
from jax.experimental import pallas as pl
from jax.experimental.pallas import tpu as pltpu
from jax.sharding import PartitionSpec as P

BF16, F32 = jnp.bfloat16, jnp.float32
NY, NH, NX, NL = 4, 4, 4, 2
LANES = 128


def id_codes(ids):
    return ((ids & 127) + 128).astype(F32) * jnp.exp2((ids >> 7).astype(F32))


def kernel(
    img_hbm, cap_ref, tax_ref, sw_ref, dw_ref, o_ref,
    img_ref, caps, img_t, codes, select, row_codes, col_codes, e_buf, e_low, t_high, t_low, acc_e, acc_t, t_sum, peaks,
    sum_out, sum_in, stat_out, stat_in,
    p_own, p_out, p_in, ya_out, ya_in, zs_out, zs_in, yf_out, yf_in, zf_out, zf_in,
    x_out, x_in, l_out, l_in,
    img_sem, cap_send, cap_recv, id_send, id_recv, sum_send, sum_recv, stat_send, stat_recv,
    p_send, p_recv, ya_send, ya_recv, zs_send, zs_recv, yf_send, yf_recv, zf_send, zf_recv,
    x_send, x_recv, l_send, l_recv,
):
    rows, width = img_ref.shape
    own = cap_ref.shape[0]
    pair = 2 * own
    ranks = tax_ref.shape[0]
    scale = width ** -0.5
    to_exp2 = scale * math.log2(math.e)

    wide, narrow = lax.axis_index("wide"), lax.axis_index("narrow")
    core, h, y = wide % 2, (wide // 2) % NH, wide // (2 * NH)
    x, low = narrow % NX, narrow // NX
    def chip(dy, dh):
        return ((y + dy) % NY) * NH + (h + dh) % NH

    def slot(dy, dh, dc=0):
        return chip(dy, dh) * 2 + (core + dc) % 2

    def at_wide(dy, dh, dc=0):
        return {"wide": slot(dy, dh, dc)}

    def at_narrow(dx, dl):
        return {"narrow": ((low + dl) % NL) * NX + (x + dx) % NX}

    img_copy = pltpu.make_async_copy(img_hbm, img_ref, img_sem.at[0])
    img_copy.start()

    barrier = pltpu.get_barrier_semaphore()
    partners = [at_wide(0, 0, 1)]
    partners += [at_wide(0, d) for d in range(1, NH)] + [at_wide(d, 0) for d in range(1, NY)]
    partners += [at_narrow(dx, dl) for dl in range(NL) for dx in range(NX) if dx or dl]
    for partner in partners:
        pl.semaphore_signal(barrier, inc=1, device_id=partner, device_id_type=pl.DeviceIdType.MESH)

    sent = []

    def send(src, dst, send_sem, recv_sem, where):
        copy = pltpu.make_async_remote_copy(
            src_ref=src, dst_ref=dst, send_sem=send_sem, recv_sem=recv_sem,
            device_id=where, device_id_type=pl.DeviceIdType.MESH,
        )
        copy.start()
        sent.append(copy)

    def arrived(dst, recv_sem):
        pltpu.make_async_copy(dst, dst, recv_sem).wait()

    pl.semaphore_wait(barrier, len(partners))

    cap_sends = iter(range(64))

    def send_caps(s, where, src=None):
        src = caps.at[s] if src is None else src
        send(src, caps.at[s], cap_send.at[next(cap_sends)], cap_recv.at[s], where)

    def caps_arrived(s):
        arrived(caps.at[s], cap_recv.at[s])

    for where in ((1, 0), (3, 0), (2, 0)):
        send_caps(wide, at_wide(*where), cap_ref)

    own_codes = id_codes(tax_ref[...])
    padded = jnp.concatenate([own_codes, jnp.zeros((8 - ranks, rows), F32)], axis=0)
    mine = pltpu.roll(padded, (rows - own * narrow) % rows, 1)[:, :LANES]
    codes[pl.ds(core, 1), pl.ds(chip(0, 0), 1)] = jnp.concatenate([mine, mine], axis=0).astype(BF16)[None, None]

    def code_part(c, first, count):
        return codes.at[c, pl.ds(first, count)]

    part = code_part(core, chip(0, 0), 1)
    for d in (1, 3, 2):
        send(part, part, id_send.at[d], id_recv.at[NH - d], at_wide(0, d))
    for where in ((0, 1), (0, 3), (0, 2), (0, 0, 1)):
        send_caps(wide, at_wide(*where), cap_ref)

    caps[pl.ds(wide, 1)] = cap_ref[...][None]
    for k in range(ranks):
        row_codes[k] = jnp.broadcast_to(own_codes[k : k + 1], (16, rows)).astype(BF16)
    t_sum[...] = jnp.zeros_like(t_sum)

    def on_y(s, places):
        for dy in places:
            send_caps(s, at_wide(dy, 0))

    def to_core(s):
        send_caps(s, at_wide(0, 0, 1))

    def targets(dy, beside=()):
        first = NH * ((y + dy) % NY)
        tiles = [[codes[c, first + i].astype(F32)[:8] for c in (0, 1)] for i in range(NH)]
        turned = [jnp.concatenate(tile, axis=0).T[:own] for tile in tiles]
        col_codes[...] = jnp.dot(
            jnp.concatenate(turned, axis=0).astype(BF16), select[...], preferred_element_type=F32
        ).astype(BF16)
        values = [jnp.full((16, 256), dw_ref[k], F32) for k in range(ranks + 1)]
        highs = [v.astype(BF16) for v in values]
        lows = [(v - w.astype(F32)).astype(BF16) for v, w in zip(values, highs)]
        size = 32

        def step(i):
            for c, j in ((c, j) for c in (0, 1) for j in range(0, rows, 256)):
                cut = slice(j, j + 256)
                small = []
                for r in range(0, own, size):
                    high = jnp.broadcast_to(highs[0][None], (size // 16, 16, 256))
                    rest = jnp.broadcast_to(lows[0][None], (size // 16, 16, 256))
                    for k in range(ranks):
                        lane = (c * ranks + k) * LANES
                        col = col_codes[pl.ds(i * own + r, size), lane : lane + LANES]
                        col = col.reshape(size // 16, 16, LANES)
                        same = jnp.concatenate([col, col], axis=2) == row_codes[k, :, cut][None]
                        high = jnp.where(same, highs[k + 1][None], high)
                        rest = jnp.where(same, lows[k + 1][None], rest)
                    t_high[2 * (first + i) + c, pl.ds(r, size), cut] = high.reshape(size, 256)
                    t_low[2 * (first + i) + c, pl.ds(r, size), cut] = rest.reshape(size, 256)
                    small += [rest[q] for q in range(size // 16)]
                while len(small) > 1:
                    small = [a + b for a, b in zip(small[::2], small[1::2])] + small[len(small) // 2 * 2 :]
                t_sum[:, cut] += small[0].astype(F32)

        for i in range(NH):
            step(i)
            if i < len(beside):
                beside[i]()
        ones = jnp.ones((16, 2 * NH * own), BF16)
        for j in range(0, rows, 256):
            cut = slice(j, j + 256)
            block = t_high[pl.ds(2 * first, 2 * NH), :, cut].reshape(2 * NH * own, 256)
            t_sum[:1, cut] += jnp.dot(ones, block, preferred_element_type=F32)[:1]

    def products(slots, biggest):
        for first, second in zip(slots[::2], slots[1::2]):
            block = jnp.concatenate([caps[first], caps[second]], axis=0)
            s = jnp.dot(block, img_t[...], preferred_element_type=F32)
            e_buf[first] = s[:own]
            e_buf[second] = s[own:]
            biggest = jnp.maximum(biggest, jnp.max(s.reshape(pair // 8, 8, rows), axis=0))
        return biggest

    def exponentials(slots, order, peak, biggest, total):
        new_peak = jnp.max(biggest, axis=0, keepdims=True)
        shrink = jnp.exp2((peak - new_peak) * to_exp2)
        part = jnp.zeros((8, rows), F32)
        for s in slots:
            e = jnp.exp2((e_buf[s] - new_peak) * to_exp2)
            e_buf[s] = e
            e_low[s] = e.astype(BF16)
            part = part + jnp.sum(e.reshape(own // 8, 8, rows), axis=0)
        peaks[order : order + 1] = new_peak
        return new_peak, shrink, total * shrink + jnp.sum(part, axis=0, keepdims=True)

    def moments(slots, shrink, first):
        turned = jnp.concatenate([caps[s] for s in slots], axis=0).T
        for j in range(0, rows, 256):
            cut = slice(j, j + 256)
            low_e = jnp.concatenate([e_low[s, :, cut] for s in slots], axis=0)
            high_t = jnp.concatenate([t_high[s, :, cut] for s in slots], axis=0)
            new_e = jnp.dot(turned, low_e, preferred_element_type=F32)
            new_t = jnp.dot(turned, high_t, preferred_element_type=F32)
            if first:
                acc_e[:, cut] = new_e
                acc_t[:, cut] = new_t
            else:
                acc_e[:, cut] = acc_e[:, cut] * shrink[:, cut] + new_e
                acc_t[:, cut] = acc_t[:, cut] + new_t

    def everyone():
        for dl in range(NL):
            for dx in range(NX):
                if dx or dl:
                    yield dl * NX + dx, ((NL - dl) % NL) * NX + (NX - dx) % NX, at_narrow(dx, dl)

    def folded(row):
        pieces = [row[:, j : j + LANES] for j in range(0, rows, LANES)]
        return jnp.concatenate(pieces + [jnp.zeros((8 - len(pieces), LANES), F32)], axis=0)

    def flat(tile):
        return jnp.concatenate([tile[i : i + 1] for i in range(rows // LANES)], axis=1)

    shape = (16, 2 * ranks * LANES)
    column, row = (lax.broadcasted_iota(jnp.int32, shape, d) for d in (1, 0))
    block = column // LANES
    select[...] = (row == block + jnp.where(block >= ranks, 8 - ranks, 0)).astype(BF16)
    img_copy.wait()
    img_t[...] = img_ref[...].T
    peak = jnp.full((1, rows), -jnp.inf, F32)
    exp_total = jnp.zeros((1, rows), F32)
    caps_arrived(slot(0, 0, 1))
    largest = [products([slot(0, 0), slot(0, 0, 1)], jnp.broadcast_to(peak, (8, rows)))]

    for d in (1, 3, 2):
        arrived(code_part(core, chip(0, d), 1), id_recv.at[d])
    part = code_part(core, NH * y, NH)
    for d in (1, 3, 2):
        send(part, part, id_send.at[NH - 1 + d], id_recv.at[NH - 1 + NY - d], at_wide(d, 0))
    send(part, part, id_send.at[7], id_recv.at[7], at_wide(0, 0, 1))
    for dh in (1, 3):
        caps_arrived(slot(0, dh))
        on_y(slot(0, dh), (1, 3))
        to_core(slot(0, dh))
    arrived(code_part(1 - core, NH * y, NH), id_recv.at[7])
    for dy in (1, 3, 2):
        caps_arrived(slot(dy, 0))
        if dy == 2:
            send_caps(slot(dy, 0), at_wide(0, 1))
            send_caps(slot(dy, 0), at_wide(0, 3))
        to_core(slot(dy, 0))
    targets(0)
    for dy in (1, 3, 2):
        part = code_part(core, NH * ((y + dy) % NY), NH)
        arrived(part, id_recv.at[NH - 1 + dy])
        send(part, part, id_send.at[7 + dy], id_recv.at[7 + dy], at_wide(0, 0, 1))
    corners = [(dy, dh) for dh in (1, 3) for dy in (1, 3)]
    first = [slot(dy, 0, dc) for dy in range(NY) for dc in (0, 1)]
    caps_arrived(slot(0, 2))
    on_y(slot(0, 2), (2, 1, 3))
    to_core(slot(0, 2))
    for dy in (1, 2, 3):
        caps_arrived(slot(dy, 0, 1))

    def pairs(slots):
        def product(two):
            largest[0] = products(two, largest[0])

        return [functools.partial(product, slots[i : i + 2]) for i in range(0, len(slots), 2)]

    def code_arrived(dy):
        arrived(code_part(1 - core, NH * ((y + dy) % NY), NH), id_recv.at[7 + dy])

    code_arrived(1)
    targets(1, pairs(first[2:]))
    peak, shrink, exp_total = exponentials(first, 0, peak, largest[0], exp_total)
    for place in corners:
        caps_arrived(slot(*place))
        to_core(slot(*place))
    column = [(0, 1), (0, 3), (0, 2)]
    second = [slot(*place, dc) for place in column + corners for dc in (0, 1)]
    for place in column:
        caps_arrived(slot(*place, 1))
    largest[0] = jnp.broadcast_to(peak, (8, rows))
    code_arrived(3)
    targets(3, pairs(second[:6]))
    code_arrived(2)
    late = [(2, 1), (2, 3), (2, 2), (1, 2), (3, 2)]
    for place in corners:
        caps_arrived(slot(*place, 1))
    targets(2, pairs(second[6:]))
    for place in late[:2]:
        caps_arrived(slot(*place))
        to_core(slot(*place))
    for place in late[2:]:
        caps_arrived(slot(*place))
        to_core(slot(*place))
    peak, shrink, exp_total = exponentials(second, 1, peak, largest[0], exp_total)
    shrinks = [shrink]
    third = [slot(*place, dc) for place in late for dc in (0, 1)]
    biggest = jnp.broadcast_to(peak, (8, rows))
    for place in late:
        caps_arrived(slot(*place, 1))
        biggest = products([slot(*place), slot(*place, 1)], biggest)
    peak, shrink, exp_total = exponentials(third, 2, peak, biggest, exp_total)
    shrinks.append(shrink)

    stat_out[...] = jnp.concatenate([folded(peak), folded(exp_total)], axis=0)
    for k, mirror, where in everyone():
        send(stat_out, stat_in.at[mirror], stat_send.at[k], stat_recv.at[mirror], where)
    sum_out[...] = folded(jnp.sum(t_sum[...], axis=0, keepdims=True))
    for k, mirror, where in everyone():
        send(sum_out, sum_in.at[mirror], sum_send.at[k], sum_recv.at[mirror], where)
    moments(first, None, True)
    moments(second, shrinks[0], False)
    for k, _, _ in everyone():
        arrived(sum_in.at[k], sum_recv.at[k])
    t_all = flat(sum_out[...] + sum(sum_in[k] for k, _, _ in everyone()))
    weight = sw_ref[...].reshape(1, rows)
    factor_t = weight / t_all
    moments(third, shrinks[1], False)
    for k, _, _ in everyone():
        arrived(stat_in.at[k], stat_recv.at[k])
    stats = [stat_out[...]] + [stat_in[k] for k, _, _ in everyone()]
    top = functools.reduce(jnp.maximum, [s[:8] for s in stats])
    exp_all = flat(sum(s[8:] * jnp.exp2((s[:8] - top) * to_exp2) for s in stats))
    top = flat(top)
    factor_e = weight / exp_all
    to_e = [factor_e * jnp.exp2((peaks[i : i + 1] - top) * to_exp2) for i in range(3)]

    def group(dy, dh):
        if dh == 0:
            return 0
        return 2 if dy == 2 or (dh == 2 and dy) else 1

    def terms(dy, dh):
        g, k = chip(dy, dh), dy * NH + dh
        grads = []
        for c in (0, 1):
            s = 2 * g + c
            target = t_high[s].astype(F32) + t_low[s].astype(F32)
            grads.append((to_e[group(dy, dh)] * e_buf[s] - factor_t * target).astype(BF16))
        p_own[k] = scale * jnp.dot(jnp.concatenate(grads, axis=0), img_ref[...], preferred_element_type=F32)
        p_out[k] = p_own[k, pl.ds((1 - core) * own, own), :].astype(BF16)
        send(p_out.at[k], p_in.at[k], p_send.at[k], p_recv.at[k], at_wide(0, 0, 1))

    def chip_sum(dy, dh):
        k = dy * NH + dh
        arrived(p_in.at[k], p_recv.at[k])
        return p_own[k, pl.ds(core * own, own), :] + p_in[k].astype(F32)

    def over_y(dy, dh):
        ya_out[dy, dh] = chip_sum(dy, dh).astype(BF16)
        send(
            ya_out.at[dy, dh], ya_in.at[NY - dy, dh], ya_send.at[dy, dh], ya_recv.at[NY - dy, dh], at_wide(dy, 0)
        )

    def over_z(dh):
        zs_out[dh] = chip_sum(2, dh).astype(BF16)
        send(zs_out.at[dh], zs_in.at[NH - dh], zs_send.at[dh], zs_recv.at[NH - dh], at_wide(0, dh))

    def last_y(dy):
        value = chip_sum(dy, 0)
        if dy == 2:
            for dh in (1, 3):
                arrived(zs_in.at[dh], zs_recv.at[dh])
                value = value + zs_in[dh].astype(F32)
        yf_out[dy] = value.astype(BF16)
        send(yf_out.at[dy], yf_in.at[NY - dy], yf_send.at[dy], yf_recv.at[NY - dy], at_wide(dy, 0))

    def last_z(dh):
        value = chip_sum(0, dh)
        for dy in (1, 3, 2) if dh == 2 else (1, 3):
            arrived(ya_in.at[dy, dh], ya_recv.at[dy, dh])
            value = value + ya_in[dy, dh].astype(F32)
        zf_out[dh] = value.astype(BF16)
        send(zf_out.at[dh], zf_in.at[NH - dh], zf_send.at[dh], zf_recv.at[NH - dh], at_wide(0, dh))

    def last():
        value = chip_sum(0, 0)
        for dy in range(1, NY):
            arrived(yf_in.at[dy], yf_recv.at[dy])
            value = value + yf_in[dy].astype(F32)
        for dh in range(1, NH):
            arrived(zf_in.at[dh], zf_recv.at[dh])
            value = value + zf_in[dh].astype(F32)
        o_ref[1] = value

    def image_terms():
        own_e = scale * factor_e * jnp.exp2((peak - top) * to_exp2)
        own_t = scale * factor_t
        turned = (acc_e[...] * own_e - acc_t[...] * own_t).T
        x_out[...] = turned.reshape(NL, NX, own, width).astype(BF16)
        for d in range(1, NX):
            to = (x + d) % NX
            send(x_out.at[:, to], x_in.at[NX - d], x_send.at[d], x_recv.at[NX - d], at_narrow(d, 0))

    def image_sum():
        for d in range(1, NX):
            arrived(x_in.at[d], x_recv.at[d])

        def total(which):
            value = x_out[which, x].astype(F32)
            for d in range(1, NX):
                value = value + x_in[d, which].astype(F32)
            return value

        l_out[...] = total(1 - low).astype(BF16)
        send(l_out, l_in, l_send.at[0], l_recv.at[0], at_narrow(0, 1))
        o_ref[0] = total(low)

    def image_finish():
        arrived(l_in, l_recv.at[0])
        o_ref[0] = o_ref[0] + l_in[...].astype(F32)

    for step in ((2, 1), (2, 3), (1, 2), (3, 2), (2, 2)):
        terms(*step)
    over_z(1)
    over_z(3)
    terms(1, 1)
    terms(3, 1)
    for dy in (1, 3, 2):
        over_y(dy, 2)
    terms(1, 3)
    terms(3, 3)
    over_y(1, 1)
    over_y(3, 1)
    image_terms()
    over_y(1, 3)
    over_y(3, 3)
    for step in ((1, 0), (3, 0), (2, 0), (0, 2), (0, 1)):
        terms(*step)
    last_y(1)
    last_y(3)
    terms(0, 3)
    terms(0, 0)
    last_z(2)
    last_y(2)
    last_z(1)
    last_z(3)
    image_sum()
    image_finish()
    last()
    for copy in sent:
        copy.wait_send()


def body(images, captions, taxon_paths, sample_weight, depth_weight):
    rows, width = images.shape
    own = captions.shape[0]
    pair = 2 * own
    ranks = taxon_paths.shape[0]
    slots = 2 * NY * NH
    chips = NY * NH
    vmem = pl.BlockSpec(memory_space=pltpu.VMEM)
    dma = pltpu.SemaphoreType.DMA
    scratch = [
        pltpu.VMEM((rows, width), BF16),
        pltpu.VMEM((slots, own, width), BF16),
        pltpu.VMEM((width, rows), BF16),
        pltpu.VMEM((2, chips, 16, LANES), BF16),
        pltpu.VMEM((16, 2 * ranks * LANES), BF16),
        pltpu.VMEM((ranks, 16, rows), BF16),
        pltpu.VMEM((NH * own, 2 * ranks * LANES), BF16),
        pltpu.VMEM((slots, own, rows), F32),
        pltpu.VMEM((slots, own, rows), BF16),
        pltpu.VMEM((slots, own, rows), BF16),
        pltpu.VMEM((slots, own, rows), BF16),
        pltpu.VMEM((width, rows), F32),
        pltpu.VMEM((width, rows), F32),
        pltpu.VMEM((16, rows), F32),
        pltpu.VMEM((8, rows), F32),
        pltpu.VMEM((8, LANES), F32),
        pltpu.VMEM((NL * NX, 8, LANES), F32),
        pltpu.VMEM((16, LANES), F32),
        pltpu.VMEM((NL * NX, 16, LANES), F32),
        pltpu.VMEM((chips, pair, width), F32),
        pltpu.VMEM((chips, own, width), BF16),
        pltpu.VMEM((chips, own, width), BF16),
        pltpu.VMEM((NY, NH, own, width), BF16),
        pltpu.VMEM((NY, NH, own, width), BF16),
        pltpu.VMEM((NH, own, width), BF16),
        pltpu.VMEM((NH, own, width), BF16),
        pltpu.VMEM((NY, own, width), BF16),
        pltpu.VMEM((NY, own, width), BF16),
        pltpu.VMEM((NH, own, width), BF16),
        pltpu.VMEM((NH, own, width), BF16),
        pltpu.VMEM((NL, NX, own, width), BF16),
        pltpu.VMEM((NX, NL, own, width), BF16),
        pltpu.VMEM((own, width), BF16),
        pltpu.VMEM((own, width), BF16),
        dma((1,)), dma((64,)), dma((slots,)), dma((12,)), dma((12,)), dma((8,)), dma((8,)), dma((8,)), dma((8,)),
        dma((chips,)), dma((chips,)), dma((NY, NH)), dma((NY, NH)), dma((NH,)), dma((NH,)),
        dma((NY,)), dma((NY,)), dma((NH,)), dma((NH,)),
        dma((NX,)), dma((NX,)), dma((1,)), dma((1,)),
    ]
    out = jax.ShapeDtypeStruct((2, own, width), F32)
    pairs = slots * own * rows
    o = pl.pallas_call(
        kernel,
        out_shape=out,
        in_specs=[pl.BlockSpec(memory_space=pl.ANY), vmem, vmem, vmem, pl.BlockSpec(memory_space=pltpu.SMEM)],
        out_specs=vmem,
        scratch_shapes=scratch,
        compiler_params=pltpu.CompilerParams(
            collective_id=0, has_side_effects=True, vmem_limit_bytes=58 * 1024 * 1024
        ),
        cost_estimate=pl.CostEstimate(
            flops=8 * pairs * width, bytes_accessed=4 * rows * width, transcendentals=pairs
        ),
    )(images, captions, taxon_paths, sample_weight, depth_weight)
    return o[0], o[1]


def solution(mesh):
    return jax.shard_map(
        body,
        mesh=mesh,
        in_specs=(P("wide", None), P(("wide", "narrow"), None), P(None, "wide"), P("wide"), P()),
        out_specs=(P(("wide", "narrow"), None), P(("wide", "narrow"), None)),
        check_vma=False,
    )
```
